256 devices in a mesh: grp: 8 (over y, z_lo), row: 32 (over z_hi, x, core).
Axes of the slice: x: 4, y: 4, z: 8 (z_hi: 4, z_lo: 2; z = z_hi * 2 + z_lo), core: 2. Of those that a mesh axis runs over, the one named last changes fastest.
Arguments:
- matrix: float32 [1048576, 256], P(('grp', 'row')), may hold values from -6 to 6
- row_signs: int32 [1048576], P(('grp', 'row')), may hold values from -1 to 1, as said below
- block_dest: int32 [8192], P(('grp', 'row')), may hold values from 0 to 15
- block_signs: int32 [8192], P(('grp', 'row')), may hold values from -1 to 1, as said below
Outputs:
- sketch: float32 [2048, 256], P('row')
The draws below stay inside these ranges and needn't reach their ends.
Inputs may be any that keep to these rules, and one draw needn't show every extreme that they name: `row_signs`: each entry is -1 or 1. `block_signs`: each entry is -1 or 1.
All inputs are finite; a program needn't handle non-finite values.
Results may differ from the reference program's by a relative error of at most 0.0003.
Values sent between devices are 32-bit elements; how exact they have to be, the bound alone decides.
No kernel may reach another device: no remote copies, remote signals or barrier semaphores. Data moves between devices by JAX's collectives and lax.ppermute only.
A program may use at most 64 MiB of HBM per device.

```python
import math
import jax
import jax.numpy as jnp
from jax import lax

C = 256
SKETCH = 2048
BLOCK = 128
R_DEV = 4096
ROWS = 1048576
NBLK = 8192
N_GRP = 8
N_ROW = 32


def draw_row_signs(key, part):
    picks = jax.random.randint(jax.random.fold_in(key, 11), (ROWS,), 0, 2, dtype=jnp.int32)
    return (2 * picks - 1).astype(jnp.int32)


def draw_block_signs(key, part):
    picks = jax.random.randint(jax.random.fold_in(key, 23), (NBLK,), 0, 2, dtype=jnp.int32)
    return (2 * picks - 1).astype(jnp.int32)


def set_ends(result, key, low, top_value):
    longest = result.shape.index(max(result.shape))
    spots = []
    for shift in (0, 1):
        where = [jax.random.randint(jax.random.fold_in(key, axis), (), 0, length) for axis, length in enumerate(result.shape)]
        where[longest] = (where[longest] + shift) % result.shape[longest]
        spots.append(tuple(where))
    return result.at[spots[0]].set(low).at[spots[1]].set(top_value)


def block_levels(rng, extent, split, low, largest):
    loudness = 1.0
    for dim, parts in split:
        heights = jax.random.uniform(jax.random.fold_in(jax.random.fold_in(rng, 6), dim), (parts,), jnp.float32, low / len(split), largest / len(split))
        loudness = loudness * jnp.repeat(jnp.exp(heights), extent[dim] // parts).reshape((-1,) + (1,) * (len(extent) - 1 - dim))
    return loudness


def noise(own_key, extent, spread, most, cuts=(), kind=jnp.bfloat16):
    array = jax.random.normal(own_key, extent, jnp.float32) * spread
    if len(cuts) > 0:
        array = block_levels(own_key, extent, cuts, -0.22, 0.18) * array
    return jnp.clip(array, min=-most, max=most).astype(kind)


def setup_inputs(seed: int = 0) -> dict:
    seeds = jax.random.split(jax.random.key(seed), 5)
    matrix = noise(seeds[0], (ROWS, C), 1.0, 6.0, ((0, 256),), jnp.float32)
    row_signs = draw_row_signs(jax.random.fold_in(seeds[4], 71), 0)
    block_dest = set_ends(jax.random.randint(seeds[2], (NBLK,), 0, SKETCH // BLOCK), jax.random.fold_in(seeds[2], 1), 0, (SKETCH // BLOCK) - 1).astype(jnp.int32)
    block_signs = draw_block_signs(jax.random.fold_in(seeds[4], 71), 0)
    return dict(matrix=matrix, row_signs=row_signs, block_dest=block_dest, block_signs=block_signs)


def sylvester(order):
    indices = jnp.arange(order, dtype=jnp.int32)
    common = indices[:, None] & indices[None, :]
    parity = jnp.zeros((order, order), jnp.int32)
    for section in range(order.bit_length() - 1):
        parity = parity + (common >> section & 1)
    return (1 - 2 * (parity % 2)).astype(jnp.float32)

def reference(matrix, row_signs, block_dest, block_signs):
    exponent = R_DEV.bit_length() - 1
    first_size = 1 << exponent // 2
    second_size = R_DEV // first_size
    precise = lax.Precision.HIGHEST
    h_device = sylvester(N_ROW)
    h_first = sylvester(first_size)
    h_second = sylvester(second_size)
    slab_rows = N_ROW * R_DEV
    blocks_slab = slab_rows // BLOCK
    targets = jnp.arange(SKETCH // BLOCK, dtype=jnp.int32)

    def one_slab(pieces):
        values, signs, dests, flips = pieces
        signed = values * signs[:, None].astype(jnp.float32)
        shaped = signed.reshape(N_ROW, first_size, second_size, C)
        shaped = jnp.einsum('xd,dabc->xabc', h_device, shaped, precision=precise)
        shaped = jnp.einsum('ya,dabc->dybc', h_first, shaped, precision=precise)
        shaped = jnp.einsum('zb,dabc->dazc', h_second, shaped, precision=precise)
        mixed = shaped.reshape(blocks_slab, BLOCK, C) / math.sqrt(slab_rows)
        routing = (dests[None, :] == targets[:, None]).astype(jnp.float32) * flips[None, :].astype(jnp.float32)
        return jnp.einsum('sn,nkc->skc', routing, mixed, precision=precise)
    partial_sums = lax.map(one_slab, (matrix.reshape(N_GRP, slab_rows, C), row_signs.reshape(N_GRP, slab_rows), block_dest.reshape(N_GRP, blocks_slab), block_signs.reshape(N_GRP, blocks_slab)))
    return lax.optimization_barrier(jnp.sum(partial_sums, axis=0)).reshape(SKETCH, C) * math.sqrt(SKETCH / ROWS)
```

```python
import functools
import math

import jax
import jax.numpy as jnp
from jax import lax
from jax.experimental import pallas as pl
from jax.experimental.pallas import tpu as pltpu
from jax.sharding import PartitionSpec as P

SKETCH = 2048
MIB = 1 << 20
AXES = ("grp", "row")


def parity(bits):
    for shift in (8, 4, 2, 1):
        bits = bits ^ bits >> shift
    return bits & 1


def hadamard_sign(rows, cols):
    return (1 - 2 * parity(rows & cols)).astype(jnp.float32)


def two_parts(value):
    high = value.astype(jnp.bfloat16)
    low = (value - high.astype(jnp.float32)).astype(jnp.bfloat16)
    return high, low


def transform_kernel(core_ref, matrix_ref, signs_ref, own_ref, send_ref):
    count, block, cols = matrix_ref.shape
    half = block // 2
    core = core_ref[0]
    out_row = lax.broadcasted_iota(jnp.int32, (block, block), 0)
    in_row = lax.broadcasted_iota(jnp.int32, (block, block), 1)
    hadamard = hadamard_sign(out_row ^ core * half, in_row)
    for unit in range(count):
        high, low = two_parts(matrix_ref[unit])
        signed = (hadamard * signs_ref[pl.ds(unit, 1), :].astype(jnp.float32)).astype(jnp.bfloat16)
        result = jnp.dot(
            jnp.concatenate([signed, signed], axis=1),
            jnp.concatenate([high, low], axis=0),
            preferred_element_type=jnp.float32,
        )
        own_ref[unit] = result[:half]
        send_ref[unit] = result[half:]


def transform(core, matrix, row_signs):
    count, block, cols = matrix.shape
    step = 8
    half = jax.ShapeDtypeStruct((count, block // 2, cols), jnp.float32)
    return pl.pallas_call(
        transform_kernel,
        grid_spec=pltpu.PrefetchScalarGridSpec(
            num_scalar_prefetch=1,
            grid=(count // step,),
            in_specs=[
                pl.BlockSpec((step, block, cols), lambda i, core: (i, 0, 0)),
                pl.BlockSpec((step, block), lambda i, core: (i, 0)),
            ],
            out_specs=[
                pl.BlockSpec((step, block // 2, cols), lambda i, core: (i, 0, 0)),
                pl.BlockSpec((step, block // 2, cols), lambda i, core: (i, 0, 0)),
            ],
        ),
        out_shape=[half, half],
        compiler_params=pltpu.CompilerParams(vmem_limit_bytes=16 * MIB),
        cost_estimate=pl.CostEstimate(flops=2 * 2 * 128 * 128 * 256 * 32, bytes_accessed=8 * MIB, transcendentals=0),
        name="transform",
    )(core, matrix, row_signs)


def mix_kernel(scale, me_ref, meta_ref, own_ref, other_ref, out_ref):
    sources, _, units = meta_ref.shape
    _, half, cols = own_ref.shape
    targets = out_ref.shape[1]
    me = me_ref[0]
    target = lax.broadcasted_iota(jnp.int32, (targets, units), 0)
    sums = [jnp.zeros((targets, units), jnp.float32) for _ in range(2)]
    for source in range(sources):
        flip = 1 - 2 * parity((me >> 1) & (source >> 1))
        dests = meta_ref[source, 0:1, :]
        signs = meta_ref[source, 1:2, :] * flip
        routed = jnp.where(dests == target, signs.astype(jnp.float32), 0.0)
        sums[source & 1] = sums[source & 1] + routed
    side = (1 - 2 * (me & 1)).astype(jnp.float32)
    wide = units * 8
    unit_row = lax.broadcasted_iota(jnp.int32, (units, wide), 0)
    unit_col = lax.broadcasted_iota(jnp.int32, (units, wide), 1)
    spread = (hadamard_sign(unit_row, unit_col >> 3) * scale).astype(jnp.bfloat16)
    keep = (lax.broadcasted_iota(jnp.int32, (targets * 8, wide), 0) & 7) == (
        lax.broadcasted_iota(jnp.int32, (targets * 8, wide), 1) & 7
    )
    highs, lows = [], []
    for total in (sums[0] + side * sums[1], sums[0] - side * sums[1]):
        tall = jnp.broadcast_to(total[:, None, :], (targets, 8, units)).reshape(targets * 8, units)
        weights = jnp.dot(tall.astype(jnp.bfloat16), spread, preferred_element_type=jnp.float32)
        high, low = two_parts(jnp.where(keep, weights, 0.0))
        highs.append(high)
        lows.append(low)
    left = jnp.concatenate(highs + highs + lows, axis=1)
    for piece in range(half // 8):
        rows = pl.ds(piece * 8, 8)
        parts = [two_parts(ref[:, rows, :].reshape(wide, cols)) for ref in (own_ref, other_ref)]
        high = [part[0] for part in parts]
        low = [part[1] for part in parts]
        result = jnp.dot(left, jnp.concatenate(high + low + high, axis=0), preferred_element_type=jnp.float32)
        out_ref[piece] = result.reshape(targets, 8, cols)


def mix(scale, me, meta, own, other, targets):
    units, half, cols = own.shape
    vmem = pl.BlockSpec(memory_space=pltpu.VMEM)
    return pl.pallas_call(
        functools.partial(mix_kernel, scale),
        in_specs=[pl.BlockSpec(memory_space=pltpu.SMEM), vmem, vmem, vmem],
        out_specs=vmem,
        out_shape=jax.ShapeDtypeStruct((half // 8, targets, 8, cols), jnp.float32),
        compiler_params=pltpu.CompilerParams(vmem_limit_bytes=24 * MIB),
        cost_estimate=pl.CostEstimate(flops=2 * 3 * 128 * 512 * 256 * 8, bytes_accessed=5 * MIB, transcendentals=0),
        name="mix",
    )(me, meta, own, other)


def body(matrix, row_signs, block_dest, block_signs):
    row_count, col_count = matrix.shape
    units = block_dest.shape[0]
    block = row_count // units
    targets = SKETCH // block
    groups = lax.axis_size("grp")
    devs = lax.axis_size("row")
    total_rows = row_count * devs * groups
    scale = math.sqrt(SKETCH / total_rows) / math.sqrt(row_count * devs)
    me = lax.axis_index("row").astype(jnp.int32).reshape(1)

    mine = jnp.stack([block_dest, block_signs])
    meta = lax.all_to_all(jnp.broadcast_to(mine[None], (devs, 2, units)), "row", 0, 0)
    own, send = transform(me & 1, matrix.reshape(units, block, col_count), row_signs.reshape(units, block))
    other = lax.ppermute(send, "row", [(i, i ^ 1) for i in range(devs)])
    partial = mix(scale, me, meta, own, other, targets)

    pieces = partial.reshape(groups * targets, 8, col_count)
    same_core = [
        [g * devs + 2 * t + core for g in range(groups) for t in range(devs // 2)] for core in range(2)
    ]
    pieces = lax.all_to_all(pieces, AXES, 0, 0, axis_index_groups=same_core)
    share = jnp.sum(pieces, axis=0)
    full = lax.all_to_all(jnp.broadcast_to(share[None], (groups, 8, col_count)), "grp", 0, 0)
    return full.reshape(groups * 8, col_count)


def solution(mesh):
    return jax.shard_map(
        body,
        mesh=mesh,
        in_specs=(P(AXES, None), P(AXES), P(AXES), P(AXES)),
        out_specs=P("row", None),
        check_vma=False,
    )
```

```python
import functools
import itertools
import math

import jax
import jax.numpy as jnp
from jax import lax
from jax.experimental import pallas as pl
from jax.experimental.pallas import tpu as pltpu
from jax.sharding import PartitionSpec as P

SKETCH = 2048
MIB = 1 << 20
AXES = ("grp", "row")


def parity(bits):
    for shift in (8, 4, 2, 1):
        bits = bits ^ bits >> shift
    return bits & 1


def hadamard_sign(rows, cols):
    return (1 - 2 * parity(rows & cols)).astype(jnp.float32)


def two_parts(value):
    high = value.astype(jnp.bfloat16)
    low = (value - high.astype(jnp.float32)).astype(jnp.bfloat16)
    return high, low


def transform_kernel(core_ref, matrix_hbm, signs_hbm, own_ref, send_ref, matrix_ref, signs_ref, sems, signs_sem):
    parts = matrix_ref.shape[0]
    step, block, cols = matrix_ref.shape[1:]
    half = block // 2
    signs_copy = pltpu.make_async_copy(signs_hbm, signs_ref, signs_sem)
    signs_copy.start()
    copies = [
        pltpu.make_async_copy(matrix_hbm.at[pl.ds(part * step, step)], matrix_ref.at[part], sems.at[part])
        for part in range(parts)
    ]
    for copy in copies:
        copy.start()
    core = core_ref[0]
    out_row = lax.broadcasted_iota(jnp.int32, (block, block), 0)
    in_row = lax.broadcasted_iota(jnp.int32, (block, block), 1)
    hadamard = hadamard_sign(out_row ^ core * half, in_row)
    signs_copy.wait()
    for part in range(parts):
        copies[part].wait()
        for place in range(step):
            unit = part * step + place
            high, low = two_parts(matrix_ref[part, place])
            signed = (hadamard * signs_ref[pl.ds(unit, 1), :].astype(jnp.float32)).astype(jnp.bfloat16)
            result = jnp.dot(
                jnp.concatenate([signed, signed], axis=1),
                jnp.concatenate([high, low], axis=0),
                preferred_element_type=jnp.float32,
            )
            own_ref[unit] = result[:half]
            send_ref[unit] = result[half:]


def transform(core, matrix, row_signs):
    count, block, cols = matrix.shape
    step = 2
    half = jax.ShapeDtypeStruct((count, block // 2, cols), jnp.float32)
    hbm = pl.BlockSpec(memory_space=pltpu.HBM)
    vmem = pl.BlockSpec(memory_space=pltpu.VMEM)
    return pl.pallas_call(
        transform_kernel,
        in_specs=[pl.BlockSpec(memory_space=pltpu.SMEM), hbm, hbm],
        out_specs=[vmem, vmem],
        out_shape=[half, half],
        scratch_shapes=[
            pltpu.VMEM((count // step, step, block, cols), jnp.float32),
            pltpu.VMEM((count, block), jnp.int32),
            pltpu.SemaphoreType.DMA((count // step,)),
            pltpu.SemaphoreType.DMA,
        ],
        compiler_params=pltpu.CompilerParams(vmem_limit_bytes=46 * MIB),
        cost_estimate=pl.CostEstimate(flops=2 * 2 * 128 * 128 * 256 * 32, bytes_accessed=8 * MIB, transcendentals=0),
        name="transform",
    )(core, matrix, row_signs)


def mix_kernel(scale, near, me_ref, meta_ref, own_ref, other_ref, *out_refs):
    sources, _, units = meta_ref.shape
    _, half, cols = own_ref.shape
    far = out_refs[0].shape[0]
    targets = near * far
    me = me_ref[0]
    place = lax.broadcasted_iota(jnp.int32, (targets, units), 0)
    target = place % far * near + (place // far + (me >> 1)) % near
    sums = [jnp.zeros((targets, units), jnp.float32) for _ in range(2)]
    for source in range(sources):
        flip = 1 - 2 * parity((me >> 1) & (source >> 1))
        dests = meta_ref[source, 0:1, :]
        signs = meta_ref[source, 1:2, :] * flip
        routed = jnp.where(dests == target, signs.astype(jnp.float32), 0.0)
        sums[source & 1] = sums[source & 1] + routed
    side = (1 - 2 * (me & 1)).astype(jnp.float32)
    wide = units * 8
    unit_row = lax.broadcasted_iota(jnp.int32, (units, wide), 0)
    unit_col = lax.broadcasted_iota(jnp.int32, (units, wide), 1)
    spread = (hadamard_sign(unit_row, unit_col >> 3) * scale).astype(jnp.bfloat16)
    keep = (lax.broadcasted_iota(jnp.int32, (targets * 8, wide), 0) & 7) == (
        lax.broadcasted_iota(jnp.int32, (targets * 8, wide), 1) & 7
    )
    highs, lows = [], []
    for total in (sums[0] + side * sums[1], sums[0] - side * sums[1]):
        tall = jnp.broadcast_to(total[:, None, :], (targets, 8, units)).reshape(targets * 8, units)
        weights = jnp.dot(tall.astype(jnp.bfloat16), spread, preferred_element_type=jnp.float32)
        high, low = two_parts(jnp.where(keep, weights, 0.0))
        highs.append(high)
        lows.append(low)
    left = jnp.concatenate(highs + highs + lows, axis=1)
    for piece in range(half // 8):
        rows = pl.ds(piece * 8, 8)
        parts = [two_parts(ref[:, rows, :].reshape(wide, cols)) for ref in (own_ref, other_ref)]
        high = [part[0] for part in parts]
        low = [part[1] for part in parts]
        result = jnp.dot(left, jnp.concatenate(high + low + high, axis=0), preferred_element_type=jnp.float32)
        result = result.reshape(near, far, 8, cols)
        for step, out_ref in enumerate(out_refs):
            out_ref[:, rows, :] = result[step]


def mix(scale, me, meta, own, other, near, far):
    units, half, cols = own.shape
    vmem = pl.BlockSpec(memory_space=pltpu.VMEM)
    return pl.pallas_call(
        functools.partial(mix_kernel, scale, near),
        in_specs=[pl.BlockSpec(memory_space=pltpu.SMEM), vmem, vmem, vmem],
        out_specs=[vmem] * near,
        out_shape=[jax.ShapeDtypeStruct((far, half, cols), jnp.float32)] * near,
        compiler_params=pltpu.CompilerParams(vmem_limit_bytes=24 * MIB),
        cost_estimate=pl.CostEstimate(flops=2 * 3 * 128 * 512 * 256 * 8, bytes_accessed=5 * MIB, transcendentals=0),
        name="mix",
    )(me, meta, own, other)


Y, Z_LOW, Z_HIGH, X, CORE = 4, 2, 4, 4, 2


def flat_index(y, z_low, z_high, x, core):
    return (((y % Y * Z_LOW + z_low) * Z_HIGH + z_high) * X + x % X) * CORE + core


def places():
    return itertools.product(range(Y), range(Z_LOW), range(Z_HIGH), range(X), range(CORE))


def shifted(value, y=0, x=0):
    pairs = [(flat_index(*p), flat_index(p[0] + y, p[1], p[2], p[3] + x, p[4])) for p in places()]
    return lax.ppermute(value, AXES, pairs)


def body(matrix, row_signs, block_dest, block_signs):
    row_count, col_count = matrix.shape
    units = block_dest.shape[0]
    block = row_count // units
    groups = lax.axis_size("grp")
    devs = lax.axis_size("row")
    total_rows = row_count * devs * groups
    scale = math.sqrt(SKETCH / total_rows) / math.sqrt(row_count * devs)
    me = lax.axis_index("row").astype(jnp.int32).reshape(1)

    mine = jnp.stack([block_dest, block_signs])
    meta = lax.all_to_all(jnp.broadcast_to(mine[None], (devs, 2, units)), "row", 0, 0)
    own, send = transform(me & 1, matrix.reshape(units, block, col_count), row_signs.reshape(units, block))
    other = lax.ppermute(send, "row", [(i, i ^ 1) for i in range(devs)])
    part, *rest = mix(scale, me, meta, own, other, X, Z_HIGH)

    got = {step: shifted(rest[step - 1], x=step) for step in (2, 1, 3)}
    part = part + got[2] + (got[1] + got[3])
    lines = [
        [flat_index(y, z_low, z_high, x, core) for z_low in range(Z_LOW) for z_high in range(Z_HIGH)]
        for y in range(Y)
        for x in range(X)
        for core in range(CORE)
    ]
    both = jnp.broadcast_to(part[None], (Z_LOW, *part.shape)).reshape(Z_LOW * Z_HIGH, *part.shape[1:])
    part = jnp.sum(lax.all_to_all(both, AXES, 0, 0, axis_index_groups=lines), axis=0)
    got = {step: shifted(part, y=step) for step in (2, 1, 3)}
    return (part + got[2]) + (got[1] + got[3])


def solution(mesh):
    return jax.shard_map(
        body,
        mesh=mesh,
        in_specs=(P(AXES, None), P(AXES), P(AXES), P(AXES)),
        out_specs=P("row", None),
        check_vma=False,
    )
```

```python
import functools
import itertools
import math

import jax
import jax.numpy as jnp
from jax import lax
from jax.experimental import pallas as pl
from jax.experimental.pallas import tpu as pltpu
from jax.sharding import PartitionSpec as P

SKETCH = 2048
MIB = 1 << 20
AHEAD = 2
AXES = ("grp", "row")


def parity(bits):
    for shift in (8, 4, 2, 1):
        bits = bits ^ bits >> shift
    return bits & 1


def hadamard_sign(rows, cols):
    return (1 - 2 * parity(rows & cols)).astype(jnp.float32)


def two_parts(value):
    high = value.astype(jnp.bfloat16)
    low = (value - high.astype(jnp.float32)).astype(jnp.bfloat16)
    return high, low


def transform_kernel(place_ref, matrix_hbm, signs_hbm, own_ref, send_ref, matrix_ref, signs_ref, sems, signs_sem):
    parts = matrix_ref.shape[0]
    step, block, cols = matrix_ref.shape[1:]
    half = block // 2
    signs_copy = pltpu.make_async_copy(signs_hbm, signs_ref, signs_sem)
    signs_copy.start()
    copies = [
        pltpu.make_async_copy(matrix_hbm.at[pl.ds(part * step, step)], matrix_ref.at[part], sems.at[part])
        for part in range(parts)
    ]
    for copy in copies[:AHEAD]:
        copy.start()
    core = place_ref[0] & 1
    out_row = lax.broadcasted_iota(jnp.int32, (block, block), 0)
    in_row = lax.broadcasted_iota(jnp.int32, (block, block), 1)
    hadamard = hadamard_sign(out_row ^ core * half, in_row)
    signs_copy.wait()
    for part in range(parts):
        copies[part].wait()
        if part + AHEAD < parts:
            copies[part + AHEAD].start()
        for place in range(step):
            unit = part * step + place
            high, low = two_parts(matrix_ref[part, place])
            signed = (hadamard * signs_ref[pl.ds(unit, 1), :].astype(jnp.float32)).astype(jnp.bfloat16)
            result = jnp.dot(
                jnp.concatenate([signed, signed], axis=1),
                jnp.concatenate([high, low], axis=0),
                preferred_element_type=jnp.float32,
            )
            own_ref[unit] = result[:half]
            send_ref[unit] = result[half:]


def transform(place, matrix, row_signs):
    count, block, cols = matrix.shape
    step = 4
    half = jax.ShapeDtypeStruct((count, block // 2, cols), jnp.float32)
    hbm = pl.BlockSpec(memory_space=pltpu.HBM)
    vmem = pl.BlockSpec(memory_space=pltpu.VMEM)
    return pl.pallas_call(
        transform_kernel,
        in_specs=[pl.BlockSpec(memory_space=pltpu.SMEM), hbm, hbm],
        out_specs=[vmem, vmem],
        out_shape=[half, half],
        scratch_shapes=[
            pltpu.VMEM((count // step, step, block, cols), jnp.float32),
            pltpu.VMEM((count, block), jnp.int32),
            pltpu.SemaphoreType.DMA((count // step,)),
            pltpu.SemaphoreType.DMA,
        ],
        compiler_params=pltpu.CompilerParams(vmem_limit_bytes=46 * MIB),
        cost_estimate=pl.CostEstimate(flops=2 * 2 * 128 * 128 * 256 * 32, bytes_accessed=8 * MIB, transcendentals=0),
        name="transform",
    )(place, matrix, row_signs)


def mix_kernel(scale, near, place_ref, meta_ref, own_ref, other_ref, *out_refs):
    _, half, cols = own_ref.shape
    _, low_count, far = out_refs[0].shape[:3]
    targets = near * far
    sources, _, units = meta_ref.shape
    me = place_ref[0] % sources
    core = me & 1
    first_x = jnp.where(core == 0, me >> 1, 0)
    first_y = jnp.where(core == 0, 0, place_ref[0] // sources // low_count)
    place = lax.broadcasted_iota(jnp.int32, (targets, units), 0)
    target = place % far * near + (place // far + first_x) % near
    sums = [jnp.zeros((targets, units), jnp.float32) for _ in range(2)]
    for source in range(sources):
        flip = 1 - 2 * parity((me >> 1) & (source >> 1))
        dests = meta_ref[source, 0:1, :]
        signs = meta_ref[source, 1:2, :] * flip
        routed = jnp.where(dests == target, signs.astype(jnp.float32), 0.0)
        sums[source & 1] = sums[source & 1] + routed
    side = (1 - 2 * (me & 1)).astype(jnp.float32)
    wide = units * 8
    unit_row = lax.broadcasted_iota(jnp.int32, (units, wide), 0)
    unit_col = lax.broadcasted_iota(jnp.int32, (units, wide), 1)
    spread = (hadamard_sign(unit_row, unit_col >> 3) * scale).astype(jnp.bfloat16)
    keep = (lax.broadcasted_iota(jnp.int32, (targets * 8, wide), 0) & 7) == (
        lax.broadcasted_iota(jnp.int32, (targets * 8, wide), 1) & 7
    )
    highs, lows = [], []
    for total in (sums[0] + side * sums[1], sums[0] - side * sums[1]):
        tall = jnp.broadcast_to(total[:, None, :], (targets, 8, units)).reshape(targets * 8, units)
        weights = jnp.dot(tall.astype(jnp.bfloat16), spread, preferred_element_type=jnp.float32)
        high, low = two_parts(jnp.where(keep, weights, 0.0))
        highs.append(high)
        lows.append(low)
    left = jnp.concatenate(highs + highs + lows, axis=1)
    for step, low_z in itertools.product(range(near), range(low_count)):
        piece = (first_y + step) % near * low_count + low_z
        rows = pl.ds(pl.multiple_of(piece * 8, 8), 8)
        parts = [two_parts(ref[:, rows, :].reshape(wide, cols)) for ref in (own_ref, other_ref)]
        high = [part[0] for part in parts]
        low = [part[1] for part in parts]
        result = jnp.dot(left, jnp.concatenate(high + low + high, axis=0), preferred_element_type=jnp.float32)
        result = result.reshape(near, far, 8, cols)

        @pl.when(core == 0)
        def _():
            for turn, out_ref in enumerate(out_refs):
                out_ref[step, low_z] = result[turn]

        @pl.when(core == 1)
        def _():
            for turn in range(near):
                out_refs[step][turn, low_z] = result[turn]


def mix(scale, place, meta, own, other, near, low_count, far):
    units, half, cols = own.shape
    vmem = pl.BlockSpec(memory_space=pltpu.VMEM)
    return pl.pallas_call(
        functools.partial(mix_kernel, scale, near),
        in_specs=[pl.BlockSpec(memory_space=pltpu.SMEM), vmem, vmem, vmem],
        out_specs=[vmem] * near,
        out_shape=[jax.ShapeDtypeStruct((near, low_count, far, 8, cols), jnp.float32)] * near,
        compiler_params=pltpu.CompilerParams(vmem_limit_bytes=24 * MIB),
        cost_estimate=pl.CostEstimate(flops=2 * 3 * 128 * 512 * 256 * 8, bytes_accessed=5 * MIB, transcendentals=0),
        name="mix",
    )(place, meta, own, other)


Y, Z_LOW, Z_HIGH, X, CORE = 4, 2, 4, 4, 2


def flat_index(y, z_low, z_high, x, core):
    return (((y % Y * Z_LOW + z_low) * Z_HIGH + z_high) * X + x % X) * CORE + core


def places():
    return itertools.product(range(Y), range(Z_LOW), range(Z_HIGH), range(X), range(CORE))


def first_shift(value, step):
    pairs = []
    for y, z_low, z_high, x, core in places():
        to = (y, z_low, z_high, x + step, core) if core == 0 else (y + step, z_low, z_high, x, core)
        pairs.append((flat_index(y, z_low, z_high, x, core), flat_index(*to)))
    return lax.ppermute(value, AXES, pairs)


def second_groups():
    groups = []
    for core, fixed in itertools.product(range(CORE), range(X)):
        members = itertools.product(range(Y), range(Z_LOW), range(Z_HIGH))
        groups.append(
            [
                flat_index(free, z_low, z_high, fixed, core) if core == 0 else flat_index(fixed, z_low, z_high, free, core)
                for free, z_low, z_high in members
            ]
        )
    return groups


def body(matrix, row_signs, block_dest, block_signs):
    row_count, col_count = matrix.shape
    units = block_dest.shape[0]
    block = row_count // units
    groups = lax.axis_size("grp")
    devs = lax.axis_size("row")
    total_rows = row_count * devs * groups
    scale = math.sqrt(SKETCH / total_rows) / math.sqrt(row_count * devs)
    place = lax.axis_index(AXES).astype(jnp.int32).reshape(1)

    mine = jnp.stack([block_dest, block_signs])
    meta = lax.all_to_all(jnp.broadcast_to(mine[None], (devs, 2, units)), "row", 0, 0)
    own, send = transform(place, matrix.reshape(units, block, col_count), row_signs.reshape(units, block))
    other = lax.ppermute(send, "row", [(i, i ^ 1) for i in range(devs)])
    part, *rest = mix(scale, place, meta, own, other, X, Z_LOW, Z_HIGH)

    got = {step: first_shift(rest[step - 1], step) for step in (2, 1, 3)}
    part = (part + got[2]) + (got[1] + got[3])
    pieces = part.reshape(-1, 8, col_count)
    pieces = lax.all_to_all(pieces, AXES, 0, 0, axis_index_groups=second_groups())
    share = jnp.sum(pieces, axis=0)
    full = lax.all_to_all(jnp.broadcast_to(share[None], (groups, 8, col_count)), "grp", 0, 0)
    return full.reshape(groups * 8, col_count)


def solution(mesh):
    return jax.shard_map(
        body,
        mesh=mesh,
        in_specs=(P(AXES, None), P(AXES), P(AXES), P(AXES)),
        out_specs=P("row", None),
        check_vma=False,
    )
```

```python
import functools
import itertools
import math

import jax
import jax.numpy as jnp
from jax import lax
from jax.experimental import pallas as pl
from jax.experimental.pallas import tpu as pltpu
from jax.sharding import PartitionSpec as P

SKETCH = 2048
MIB = 1 << 20
OWN = 400
AXES = ("grp", "row")


def parity(bits):
    for shift in (8, 4, 2, 1):
        bits = bits ^ bits >> shift
    return bits & 1


def hadamard_sign(rows, cols):
    return (1 - 2 * parity(rows & cols)).astype(jnp.float32)


def two_parts(value):
    high = value.astype(jnp.bfloat16)
    low = (value - high.astype(jnp.float32)).astype(jnp.bfloat16)
    return high, low


def transform_kernel(other, place_ref, matrix_ref, signs_ref, out_ref):
    count, block, cols = matrix_ref.shape
    half = block // 2
    side = (place_ref[0] & 1) ^ other
    out_row = lax.broadcasted_iota(jnp.int32, (half, block), 0) + side * half
    in_row = lax.broadcasted_iota(jnp.int32, (half, block), 1)
    hadamard = hadamard_sign(out_row, in_row)
    for unit in range(count):
        high, low = two_parts(matrix_ref[unit])
        signed = (hadamard * signs_ref[pl.ds(unit, 1), :].astype(jnp.float32)).astype(jnp.bfloat16)
        out_ref[unit] = jnp.dot(
            jnp.concatenate([signed, signed], axis=1),
            jnp.concatenate([high, low], axis=0),
            preferred_element_type=jnp.float32,
        )


def transform(other, place, matrix, row_signs):
    count, block, cols = matrix.shape
    step = 8
    return pl.pallas_call(
        functools.partial(transform_kernel, other),
        grid_spec=pltpu.PrefetchScalarGridSpec(
            num_scalar_prefetch=1,
            grid=(count // step,),
            in_specs=[
                pl.BlockSpec((step, block, cols), lambda i, place: (i, 0, 0)),
                pl.BlockSpec((step, block), lambda i, place: (i, 0)),
            ],
            out_specs=pl.BlockSpec((step, block // 2, cols), lambda i, place: (i, 0, 0)),
        ),
        out_shape=jax.ShapeDtypeStruct((count, block // 2, cols), jnp.float32),
        compiler_params=pltpu.CompilerParams(vmem_limit_bytes=16 * MIB),
        cost_estimate=pl.CostEstimate(flops=10**9, bytes_accessed=6 * MIB, transcendentals=0),
        name="transform_other" if other else "transform_own",
    )(place, matrix, row_signs)


def add_products(place, left, half_ref, base_ref, out_ref):
    near, _, low_count, far, rows, cols = out_ref.shape
    wide = half_ref.shape[0] * rows
    core, first_y = place
    for step, low_z in itertools.product(range(near), range(low_count)):
        piece = (first_y + step) % near * low_count + low_z
        high, low = two_parts(half_ref[:, pl.ds(pl.multiple_of(piece * rows, rows), rows), :].reshape(wide, cols))
        result = jnp.dot(left, jnp.concatenate([high, low, high], axis=0), preferred_element_type=jnp.float32)
        result = result.reshape(near, far, rows, cols)
        for turn in range(near):
            to = (jnp.where(core == 0, turn, step), jnp.where(core == 0, step, turn), low_z)
            out_ref[to] = result[turn] if base_ref is None else base_ref[to] + result[turn]


def placing(place_ref, near, low_count, sources):
    me = place_ref[0] % sources
    core = me & 1
    first_x = jnp.where(core == 0, me >> 1, 0)
    first_y = jnp.where(core == 0, 0, place_ref[0] // sources // low_count)
    return me, core, first_x, first_y


def mix_own_kernel(scale, place_ref, meta_ref, own_ref, out_ref, left_ref):
    near, _, low_count, far, rows, _ = out_ref.shape
    sources, _, units = meta_ref.shape
    targets = near * far
    me, core, first_x, first_y = placing(place_ref, near, low_count, sources)
    index = lax.broadcasted_iota(jnp.int32, (targets, units), 0)
    target = index % far * near + (index // far + first_x) % near
    sums = [jnp.zeros((targets, units), jnp.float32) for _ in range(2)]
    for source in range(sources):
        flip = 1 - 2 * parity((me >> 1) & (source >> 1))
        dests = meta_ref[source, 0:1, :]
        signs = meta_ref[source, 1:2, :] * flip
        routed = jnp.where(dests == target, signs.astype(jnp.float32), 0.0)
        sums[source & 1] = sums[source & 1] + routed
    side = (1 - 2 * core).astype(jnp.float32)
    tall, wide = targets * rows, units * rows
    unit_row = lax.broadcasted_iota(jnp.int32, (units, wide), 0)
    unit_col = lax.broadcasted_iota(jnp.int32, (units, wide), 1)
    spread = (hadamard_sign(unit_row, unit_col // rows) * scale).astype(jnp.bfloat16)
    keep = lax.broadcasted_iota(jnp.int32, (tall, wide), 0) % rows == lax.broadcasted_iota(jnp.int32, (tall, wide), 1) % rows
    lefts = []
    for total in (sums[0] + side * sums[1], sums[0] - side * sums[1]):
        total = jnp.broadcast_to(total[:, None, :], (targets, rows, units)).reshape(tall, units)
        weights = jnp.dot(total.astype(jnp.bfloat16), spread, preferred_element_type=jnp.float32)
        high, low = two_parts(jnp.where(keep, weights, 0.0))
        lefts.append(jnp.concatenate([high, high, low], axis=1))
    left_ref[...] = lefts[1]
    add_products((core, first_y), lefts[0], own_ref, None, out_ref)


def mix_other_kernel(sources, place_ref, left_ref, other_ref, base_ref, out_ref):
    near, _, low_count = out_ref.shape[:3]
    _, core, _, first_y = placing(place_ref, near, low_count, sources)
    add_products((core, first_y), left_ref[...], other_ref, base_ref, out_ref)


def mix_own(scale, place, meta, own, near, low_count, far):
    units, half, cols = own.shape
    rows = half // (near * low_count)
    vmem = pl.BlockSpec(memory_space=pltpu.VMEM)
    return pl.pallas_call(
        functools.partial(mix_own_kernel, scale),
        in_specs=[pl.BlockSpec(memory_space=pltpu.SMEM), vmem, vmem],
        out_specs=[vmem, vmem],
        out_shape=[
            jax.ShapeDtypeStruct((near, near, low_count, far, rows, cols), jnp.float32),
            jax.ShapeDtypeStruct((near * far * rows, 3 * units * rows), jnp.bfloat16),
        ],
        compiler_params=pltpu.CompilerParams(vmem_limit_bytes=16 * MIB),
        cost_estimate=pl.CostEstimate(flops=OWN * 10**9, bytes_accessed=3 * MIB, transcendentals=0),
        name="mix_own",
    )(place, meta, own)


def mix_other(sources, place, left, other, base):
    vmem = pl.BlockSpec(memory_space=pltpu.VMEM)
    return pl.pallas_call(
        functools.partial(mix_other_kernel, sources),
        in_specs=[pl.BlockSpec(memory_space=pltpu.SMEM), vmem, vmem, vmem],
        out_specs=vmem,
        out_shape=jax.ShapeDtypeStruct(base.shape, jnp.float32),
        compiler_params=pltpu.CompilerParams(vmem_limit_bytes=16 * MIB),
        cost_estimate=pl.CostEstimate(flops=10**9, bytes_accessed=4 * MIB, transcendentals=0),
        name="mix_other",
    )(place, left, other, base)


Y, Z_LOW, Z_HIGH, X, CORE = 4, 2, 4, 4, 2


def flat_index(y, z_low, z_high, x, core):
    return (((y % Y * Z_LOW + z_low) * Z_HIGH + z_high) * X + x % X) * CORE + core


def places():
    return itertools.product(range(Y), range(Z_LOW), range(Z_HIGH), range(X), range(CORE))


def first_shift(value, step):
    pairs = []
    for y, z_low, z_high, x, core in places():
        to = (y, z_low, z_high, x + step, core) if core == 0 else (y + step, z_low, z_high, x, core)
        pairs.append((flat_index(y, z_low, z_high, x, core), flat_index(*to)))
    return lax.ppermute(value, AXES, pairs)


def second_groups():
    groups = []
    for core, fixed in itertools.product(range(CORE), range(X)):
        members = itertools.product(range(Y), range(Z_LOW), range(Z_HIGH))
        groups.append(
            [
                flat_index(free, z_low, z_high, fixed, core) if core == 0 else flat_index(fixed, z_low, z_high, free, core)
                for free, z_low, z_high in members
            ]
        )
    return groups


def body(matrix, row_signs, block_dest, block_signs):
    row_count, col_count = matrix.shape
    units = block_dest.shape[0]
    block = row_count // units
    groups = lax.axis_size("grp")
    devs = lax.axis_size("row")
    total_rows = row_count * devs * groups
    scale = math.sqrt(SKETCH / total_rows) / math.sqrt(row_count * devs)
    place = lax.axis_index(AXES).astype(jnp.int32).reshape(1)

    mine = jnp.stack([block_dest, block_signs])
    meta = lax.all_to_all(jnp.broadcast_to(mine[None], (devs, 2, units)), "row", 0, 0)
    matrix = matrix.reshape(units, block, col_count)
    row_signs = row_signs.reshape(units, block)
    own, send = (transform(other, place, matrix, row_signs) for other in range(2))
    other = lax.ppermute(send, "row", [(i, i ^ 1) for i in range(devs)])
    base, left = mix_own(scale, place, meta, own, X, Z_LOW, Z_HIGH)
    parts = mix_other(devs, place, left, other, base)

    got = {step: first_shift(parts[step], step) for step in (2, 1, 3)}
    part = (parts[0] + got[2]) + (got[1] + got[3])
    pieces = part.reshape(-1, 8, col_count)
    pieces = lax.all_to_all(pieces, AXES, 0, 0, axis_index_groups=second_groups())
    share = jnp.sum(pieces, axis=0)
    full = lax.all_to_all(jnp.broadcast_to(share[None], (groups, 8, col_count)), "grp", 0, 0)
    return full.reshape(groups * 8, col_count)


def solution(mesh):
    return jax.shard_map(
        body,
        mesh=mesh,
        in_specs=(P(AXES, None), P(AXES), P(AXES), P(AXES)),
        out_specs=P("row", None),
        check_vma=False,
    )
```

```python
import functools
import itertools
import math

import jax
import jax.numpy as jnp
from jax import lax
from jax.experimental import pallas as pl
from jax.experimental.pallas import tpu as pltpu
from jax.sharding import PartitionSpec as P

SKETCH = 2048
MIB = 1 << 20
AXES = ("grp", "row")


def parity(bits):
    for shift in (8, 4, 2, 1):
        bits = bits ^ bits >> shift
    return bits & 1


def hadamard_sign(rows, cols):
    return (1 - 2 * parity(rows & cols)).astype(jnp.float32)


def two_parts(value):
    high = value.astype(jnp.bfloat16)
    low = (value - high.astype(jnp.float32)).astype(jnp.bfloat16)
    return high, low


def transform_kernel(place_ref, matrix_ref, signs_ref, own_ref, send_ref):
    count, block, cols = matrix_ref.shape
    half = block // 2
    core = place_ref[0] & 1
    out_row = lax.broadcasted_iota(jnp.int32, (block, block), 0)
    in_row = lax.broadcasted_iota(jnp.int32, (block, block), 1)
    hadamard = hadamard_sign(out_row ^ core * half, in_row)
    for unit in range(count):
        high, low = two_parts(matrix_ref[unit])
        signed = (hadamard * signs_ref[pl.ds(unit, 1), :].astype(jnp.float32)).astype(jnp.bfloat16)
        result = jnp.dot(
            jnp.concatenate([signed, signed], axis=1),
            jnp.concatenate([high, low], axis=0),
            preferred_element_type=jnp.float32,
        )
        own_ref[unit] = result[:half]
        send_ref[unit] = result[half:]


def transform(place, matrix, row_signs):
    count, block, cols = matrix.shape
    step = 8
    half = jax.ShapeDtypeStruct((count, block // 2, cols), jnp.float32)
    return pl.pallas_call(
        transform_kernel,
        grid_spec=pltpu.PrefetchScalarGridSpec(
            num_scalar_prefetch=1,
            grid=(count // step,),
            in_specs=[
                pl.BlockSpec((step, block, cols), lambda i, place: (i, 0, 0)),
                pl.BlockSpec((step, block), lambda i, place: (i, 0)),
            ],
            out_specs=[
                pl.BlockSpec((step, block // 2, cols), lambda i, place: (i, 0, 0)),
                pl.BlockSpec((step, block // 2, cols), lambda i, place: (i, 0, 0)),
            ],
        ),
        out_shape=[half, half],
        compiler_params=pltpu.CompilerParams(vmem_limit_bytes=16 * MIB),
        cost_estimate=pl.CostEstimate(flops=2 * 2 * 128 * 128 * 256 * 32, bytes_accessed=8 * MIB, transcendentals=0),
        name="transform",
    )(place, matrix, row_signs)


def mix_kernel(scale, place_ref, meta_ref, own_ref, other_ref, out_ref):
    near, _, low_count, far, rows, cols = out_ref.shape
    sources, _, units = meta_ref.shape
    targets = near * far
    me = place_ref[0] % sources
    core = me & 1
    first_x = jnp.where(core == 0, me >> 1, 0)
    first_y = jnp.where(core == 0, 0, place_ref[0] // sources // low_count)
    index = lax.broadcasted_iota(jnp.int32, (targets, units), 0)
    target = index % far * near + (index // far + first_x) % near
    sums = [jnp.zeros((targets, units), jnp.float32) for _ in range(2)]
    for source in range(sources):
        flip = 1 - 2 * parity((me >> 1) & (source >> 1))
        dests = meta_ref[source, 0:1, :]
        signs = meta_ref[source, 1:2, :] * flip
        routed = jnp.where(dests == target, signs.astype(jnp.float32), 0.0)
        sums[source & 1] = sums[source & 1] + routed
    side = (1 - 2 * core).astype(jnp.float32)
    tall, wide = targets * rows, units * rows
    unit_row = lax.broadcasted_iota(jnp.int32, (units, wide), 0)
    unit_col = lax.broadcasted_iota(jnp.int32, (units, wide), 1)
    spread = (hadamard_sign(unit_row, unit_col // rows) * scale).astype(jnp.bfloat16)
    keep = lax.broadcasted_iota(jnp.int32, (tall, wide), 0) % rows == lax.broadcasted_iota(jnp.int32, (tall, wide), 1) % rows
    highs, lows = [], []
    for total in (sums[0] + side * sums[1], sums[0] - side * sums[1]):
        total = jnp.broadcast_to(total[:, None, :], (targets, rows, units)).reshape(tall, units)
        weights = jnp.dot(total.astype(jnp.bfloat16), spread, preferred_element_type=jnp.float32)
        high, low = two_parts(jnp.where(keep, weights, 0.0))
        highs.append(high)
        lows.append(low)
    left = jnp.concatenate(highs + highs + lows, axis=1)
    for step, low_z in itertools.product(range(near), range(low_count)):
        piece = (first_y + step) % near * low_count + low_z
        span = pl.ds(pl.multiple_of(piece * rows, rows), rows)
        parts = [two_parts(ref[:, span, :].reshape(wide, cols)) for ref in (own_ref, other_ref)]
        high = [part[0] for part in parts]
        low = [part[1] for part in parts]
        result = jnp.dot(left, jnp.concatenate(high + low + high, axis=0), preferred_element_type=jnp.float32)
        result = result.reshape(near, far, rows, cols)
        for turn in range(near):
            out_ref[jnp.where(core == 0, turn, step), jnp.where(core == 0, step, turn), low_z] = result[turn]


def mix(scale, place, meta, own, other, near, low_count, far):
    units, half, cols = own.shape
    rows = half // (near * low_count)
    vmem = pl.BlockSpec(memory_space=pltpu.VMEM)
    return pl.pallas_call(
        functools.partial(mix_kernel, scale),
        in_specs=[pl.BlockSpec(memory_space=pltpu.SMEM), vmem, vmem, vmem],
        out_specs=vmem,
        out_shape=jax.ShapeDtypeStruct((near, near, low_count, far, rows, cols), jnp.float32),
        compiler_params=pltpu.CompilerParams(vmem_limit_bytes=24 * MIB),
        cost_estimate=pl.CostEstimate(flops=2 * 3 * 128 * 512 * 256 * 8, bytes_accessed=5 * MIB, transcendentals=0),
        name="mix",
    )(place, meta, own, other)


Y, Z_LOW, Z_HIGH, X, CORE = 4, 2, 4, 4, 2


def flat_index(y, z_low, z_high, x, core):
    return (((y % Y * Z_LOW + z_low) * Z_HIGH + z_high) * X + x % X) * CORE + core


def places():
    return itertools.product(range(Y), range(Z_LOW), range(Z_HIGH), range(X), range(CORE))


def first_shift(value, step):
    pairs = []
    for y, z_low, z_high, x, core in places():
        to = (y, z_low, z_high, x + step, core) if core == 0 else (y + step, z_low, z_high, x, core)
        pairs.append((flat_index(y, z_low, z_high, x, core), flat_index(*to)))
    return lax.ppermute(value, AXES, pairs)


def second_groups():
    groups = []
    for core, fixed in itertools.product(range(CORE), range(X)):
        members = itertools.product(range(Y), range(Z_LOW), range(Z_HIGH))
        groups.append(
            [
                flat_index(free, z_low, z_high, fixed, core) if core == 0 else flat_index(fixed, z_low, z_high, free, core)
                for free, z_low, z_high in members
            ]
        )
    return groups


def body(matrix, row_signs, block_dest, block_signs):
    row_count, col_count = matrix.shape
    units = block_dest.shape[0]
    block = row_count // units
    groups = lax.axis_size("grp")
    devs = lax.axis_size("row")
    total_rows = row_count * devs * groups
    scale = math.sqrt(SKETCH / total_rows) / math.sqrt(row_count * devs)
    place = lax.axis_index(AXES).astype(jnp.int32).reshape(1)

    mine = jnp.stack([block_dest, block_signs])
    meta = lax.all_to_all(jnp.broadcast_to(mine[None], (devs, 2, units)), "row", 0, 0)
    matrix = matrix.reshape(units, block, col_count)
    row_signs = row_signs.reshape(units, block)
    own, send = transform(place, matrix, row_signs)
    other = lax.ppermute(send, "row", [(i, i ^ 1) for i in range(devs)])
    parts = mix(scale, place, meta, own, other, X, Z_LOW, Z_HIGH)

    got = {step: first_shift(parts[step], step) for step in (2, 1, 3)}
    part = (parts[0] + got[2]) + (got[1] + got[3])
    pieces = part.reshape(-1, 8, col_count)
    pieces = lax.all_to_all(pieces, AXES, 0, 0, axis_index_groups=second_groups())
    share = jnp.sum(pieces, axis=0)
    full = lax.all_to_all(jnp.broadcast_to(share[None], (groups, 8, col_count)), "grp", 0, 0)
    return full.reshape(groups * 8, col_count)


def solution(mesh):
    return jax.shard_map(
        body,
        mesh=mesh,
        in_specs=(P(AXES, None), P(AXES), P(AXES), P(AXES)),
        out_specs=P("row", None),
        check_vma=False,
    )
```

```python
import functools
import itertools
import math

import jax
import jax.numpy as jnp
from jax import lax
from jax.experimental import pallas as pl
from jax.experimental.pallas import tpu as pltpu
from jax.sharding import PartitionSpec as P

SKETCH = 2048
MIB = 1 << 20
AXES = ("grp", "row")


def parity(bits):
    for shift in (8, 4, 2, 1):
        bits = bits ^ bits >> shift
    return bits & 1


def hadamard_sign(rows, cols):
    return (1 - 2 * parity(rows & cols)).astype(jnp.float32)


def two_parts(value):
    high = value.astype(jnp.bfloat16)
    low = (value - high.astype(jnp.float32)).astype(jnp.bfloat16)
    return high, low


def transform_kernel(place_ref, matrix_hbm, signs_ref, own_ref, send_ref, matrix_ref, sems):
    parts, step, block, _ = matrix_ref.shape
    half = block // 2
    copies = [
        pltpu.make_async_copy(matrix_hbm.at[pl.ds(part * step, step)], matrix_ref.at[part], sems.at[part])
        for part in range(parts)
    ]
    for copy in copies:
        copy.start()
    core = place_ref[0] & 1
    out_row = lax.broadcasted_iota(jnp.int32, (block, block), 0)
    in_row = lax.broadcasted_iota(jnp.int32, (block, block), 1)
    hadamard = hadamard_sign(out_row ^ core * half, in_row)
    for part in range(parts):
        copies[part].wait()
        for place in range(step):
            unit = part * step + place
            high, low = two_parts(matrix_ref[part, place])
            signed = (hadamard * signs_ref[pl.ds(unit, 1), :].astype(jnp.float32)).astype(jnp.bfloat16)
            result = jnp.dot(
                jnp.concatenate([signed, signed], axis=1),
                jnp.concatenate([high, low], axis=0),
                preferred_element_type=jnp.float32,
            )
            own_ref[unit] = result[:half]
            send_ref[unit] = result[half:]


def transform(place, matrix, row_signs):
    count, block, cols = matrix.shape
    parts = 4
    half = jax.ShapeDtypeStruct((count, block // 2, cols), jnp.float32)
    vmem = pl.BlockSpec(memory_space=pltpu.VMEM)
    return pl.pallas_call(
        transform_kernel,
        in_specs=[pl.BlockSpec(memory_space=pltpu.SMEM), pl.BlockSpec(memory_space=pltpu.HBM), vmem],
        out_specs=[vmem, vmem],
        out_shape=[half, half],
        scratch_shapes=[
            pltpu.VMEM((parts, count // parts, block, cols), jnp.float32),
            pltpu.SemaphoreType.DMA((parts,)),
        ],
        compiler_params=pltpu.CompilerParams(vmem_limit_bytes=46 * MIB),
        cost_estimate=pl.CostEstimate(flops=2 * 2 * 128 * 128 * 256 * 32, bytes_accessed=8 * MIB, transcendentals=0),
        name="transform",
    )(place, matrix, row_signs)


def mix_kernel(scale, place_ref, meta_ref, own_ref, other_ref, out_ref):
    near, _, low_count, far, rows, cols = out_ref.shape
    sources, _, units = meta_ref.shape
    targets = near * far
    me = place_ref[0] % sources
    core = me & 1
    first_x = jnp.where(core == 0, me >> 1, 0)
    first_y = jnp.where(core == 0, 0, place_ref[0] // sources // low_count)
    index = lax.broadcasted_iota(jnp.int32, (targets, units), 0)
    target = index % far * near + (index // far + first_x) % near
    sums = [jnp.zeros((targets, units), jnp.float32) for _ in range(2)]
    for source in range(sources):
        flip = 1 - 2 * parity((me >> 1) & (source >> 1))
        dests = meta_ref[source, 0:1, :]
        signs = meta_ref[source, 1:2, :] * flip
        routed = jnp.where(dests == target, signs.astype(jnp.float32), 0.0)
        sums[source & 1] = sums[source & 1] + routed
    side = (1 - 2 * core).astype(jnp.float32)
    tall, wide = targets * rows, units * rows
    unit_row = lax.broadcasted_iota(jnp.int32, (units, wide), 0)
    unit_col = lax.broadcasted_iota(jnp.int32, (units, wide), 1)
    spread = (hadamard_sign(unit_row, unit_col // rows) * scale).astype(jnp.bfloat16)
    keep = lax.broadcasted_iota(jnp.int32, (tall, wide), 0) % rows == lax.broadcasted_iota(jnp.int32, (tall, wide), 1) % rows
    highs, lows = [], []
    for total in (sums[0] + side * sums[1], sums[0] - side * sums[1]):
        total = jnp.broadcast_to(total[:, None, :], (targets, rows, units)).reshape(tall, units)
        weights = jnp.dot(total.astype(jnp.bfloat16), spread, preferred_element_type=jnp.float32)
        high, low = two_parts(jnp.where(keep, weights, 0.0))
        highs.append(high)
        lows.append(low)
    left = jnp.concatenate(highs + highs + lows, axis=1)
    for step, low_z in itertools.product(range(near), range(low_count)):
        piece = (first_y + step) % near * low_count + low_z
        span = pl.ds(pl.multiple_of(piece * rows, rows), rows)
        parts = [two_parts(ref[:, span, :].reshape(wide, cols)) for ref in (own_ref, other_ref)]
        high = [part[0] for part in parts]
        low = [part[1] for part in parts]
        result = jnp.dot(left, jnp.concatenate(high + low + high, axis=0), preferred_element_type=jnp.float32)
        result = result.reshape(near, far, rows, cols)
        for turn in range(near):
            out_ref[jnp.where(core == 0, turn, step), jnp.where(core == 0, step, turn), low_z] = result[turn]


def mix(scale, place, meta, own, other, near, low_count, far):
    units, half, cols = own.shape
    rows = half // (near * low_count)
    vmem = pl.BlockSpec(memory_space=pltpu.VMEM)
    return pl.pallas_call(
        functools.partial(mix_kernel, scale),
        in_specs=[pl.BlockSpec(memory_space=pltpu.SMEM), vmem, vmem, vmem],
        out_specs=vmem,
        out_shape=jax.ShapeDtypeStruct((near, near, low_count, far, rows, cols), jnp.float32),
        compiler_params=pltpu.CompilerParams(vmem_limit_bytes=24 * MIB),
        cost_estimate=pl.CostEstimate(flops=2 * 3 * 128 * 512 * 256 * 8, bytes_accessed=5 * MIB, transcendentals=0),
        name="mix",
    )(place, meta, own, other)


Y, Z_LOW, Z_HIGH, X, CORE = 4, 2, 4, 4, 2


def flat_index(y, z_low, z_high, x, core):
    return (((y % Y * Z_LOW + z_low) * Z_HIGH + z_high) * X + x % X) * CORE + core


def places():
    return itertools.product(range(Y), range(Z_LOW), range(Z_HIGH), range(X), range(CORE))


def first_shift(value, step):
    pairs = []
    for y, z_low, z_high, x, core in places():
        to = (y, z_low, z_high, x + step, core) if core == 0 else (y + step, z_low, z_high, x, core)
        pairs.append((flat_index(y, z_low, z_high, x, core), flat_index(*to)))
    return lax.ppermute(value, AXES, pairs)


def second_groups():
    groups = []
    for core, fixed in itertools.product(range(CORE), range(X)):
        members = itertools.product(range(Y), range(Z_LOW), range(Z_HIGH))
        groups.append(
            [
                flat_index(free, z_low, z_high, fixed, core) if core == 0 else flat_index(fixed, z_low, z_high, free, core)
                for free, z_low, z_high in members
            ]
        )
    return groups


def body(matrix, row_signs, block_dest, block_signs):
    row_count, col_count = matrix.shape
    units = block_dest.shape[0]
    block = row_count // units
    groups = lax.axis_size("grp")
    devs = lax.axis_size("row")
    total_rows = row_count * devs * groups
    scale = math.sqrt(SKETCH / total_rows) / math.sqrt(row_count * devs)
    place = lax.axis_index(AXES).astype(jnp.int32).reshape(1)

    mine = jnp.stack([block_dest, block_signs])
    meta = lax.all_to_all(jnp.broadcast_to(mine[None], (devs, 2, units)), "row", 0, 0)
    matrix = matrix.reshape(units, block, col_count)
    row_signs = row_signs.reshape(units, block)
    own, send = transform(place, matrix, row_signs)
    other = lax.ppermute(send, "row", [(i, i ^ 1) for i in range(devs)])
    parts = mix(scale, place, meta, own, other, X, Z_LOW, Z_HIGH)

    got = {step: first_shift(parts[step], step) for step in (2, 1, 3)}
    part = (parts[0] + got[2]) + (got[1] + got[3])
    pieces = part.reshape(-1, 8, col_count)
    pieces = lax.all_to_all(pieces, AXES, 0, 0, axis_index_groups=second_groups())
    share = jnp.sum(pieces, axis=0)
    full = lax.all_to_all(jnp.broadcast_to(share[None], (groups, 8, col_count)), "grp", 0, 0)
    return full.reshape(groups * 8, col_count)


def solution(mesh):
    return jax.shard_map(
        body,
        mesh=mesh,
        in_specs=(P(AXES, None), P(AXES), P(AXES), P(AXES)),
        out_specs=P("row", None),
        check_vma=False,
    )
```

```python
import functools
import itertools
import math

import jax
import jax.numpy as jnp
from jax import lax
from jax.experimental import pallas as pl
from jax.experimental.pallas import tpu as pltpu
from jax.sharding import PartitionSpec as P

SKETCH = 2048
MIB = 1 << 20
AXES = ("grp", "row")


def parity(bits):
    for shift in (8, 4, 2, 1):
        bits = bits ^ bits >> shift
    return bits & 1


def hadamard_sign(rows, cols):
    return (1 - 2 * parity(rows & cols)).astype(jnp.float32)


def two_parts(value):
    high = value.astype(jnp.bfloat16)
    low = (value - high.astype(jnp.float32)).astype(jnp.bfloat16)
    return high, low


def transform_kernel(place_ref, matrix_hbm, signs_hbm, own_ref, send_ref, matrix_ref, signs_ref, sems, signs_sem):
    parts, step, block, _ = matrix_ref.shape
    half = block // 2
    signs_copy = pltpu.make_async_copy(signs_hbm, signs_ref, signs_sem)
    signs_copy.start()
    copies = [
        pltpu.make_async_copy(matrix_hbm.at[pl.ds(part * step, step)], matrix_ref.at[part], sems.at[part])
        for part in range(parts)
    ]
    for copy in copies:
        copy.start()
    core = place_ref[0] & 1
    out_row = lax.broadcasted_iota(jnp.int32, (block, block), 0)
    in_row = lax.broadcasted_iota(jnp.int32, (block, block), 1)
    hadamard = hadamard_sign(out_row ^ core * half, in_row)
    signs_copy.wait()
    for part in range(parts):
        copies[part].wait()
        for place in range(step):
            unit = part * step + place
            high, low = two_parts(matrix_ref[part, place])
            signed = (hadamard * signs_ref[pl.ds(unit, 1), :].astype(jnp.float32)).astype(jnp.bfloat16)
            result = jnp.dot(
                jnp.concatenate([signed, signed], axis=1),
                jnp.concatenate([high, low], axis=0),
                preferred_element_type=jnp.float32,
            )
            own_ref[unit] = result[:half]
            send_ref[unit] = result[half:]


def transform(place, matrix, row_signs):
    count, block, cols = matrix.shape
    parts = 4
    half = jax.ShapeDtypeStruct((count, block // 2, cols), jnp.float32)
    hbm = pl.BlockSpec(memory_space=pltpu.HBM)
    vmem = pl.BlockSpec(memory_space=pltpu.VMEM)
    return pl.pallas_call(
        transform_kernel,
        in_specs=[pl.BlockSpec(memory_space=pltpu.SMEM), hbm, hbm],
        out_specs=[vmem, vmem],
        out_shape=[half, half],
        scratch_shapes=[
            pltpu.VMEM((parts, count // parts, block, cols), jnp.float32),
            pltpu.VMEM((count, block), jnp.int32),
            pltpu.SemaphoreType.DMA((parts,)),
            pltpu.SemaphoreType.DMA,
        ],
        compiler_params=pltpu.CompilerParams(vmem_limit_bytes=16 * MIB),
        cost_estimate=pl.CostEstimate(flops=2 * 2 * 128 * 128 * 256 * 32, bytes_accessed=8 * MIB, transcendentals=0),
        name="transform",
    )(place, pltpu.with_memory_space_constraint(matrix, pltpu.HBM), pltpu.with_memory_space_constraint(row_signs, pltpu.HBM))


def mix_kernel(scale, place_ref, meta_ref, own_ref, other_ref, out_ref):
    near, _, low_count, far, rows, cols = out_ref.shape
    sources, _, units = meta_ref.shape
    targets = near * far
    me = place_ref[0] % sources
    core = me & 1
    first_x = jnp.where(core == 0, me >> 1, 0)
    first_y = jnp.where(core == 0, 0, place_ref[0] // sources // low_count)
    index = lax.broadcasted_iota(jnp.int32, (targets, units), 0)
    target = index % far * near + (index // far + first_x) % near
    sums = [jnp.zeros((targets, units), jnp.float32) for _ in range(2)]
    for source in range(sources):
        flip = 1 - 2 * parity((me >> 1) & (source >> 1))
        dests = meta_ref[source, 0:1, :]
        signs = meta_ref[source, 1:2, :] * flip
        routed = jnp.where(dests == target, signs.astype(jnp.float32), 0.0)
        sums[source & 1] = sums[source & 1] + routed
    side = (1 - 2 * core).astype(jnp.float32)
    tall, wide = targets * rows, units * rows
    unit_row = lax.broadcasted_iota(jnp.int32, (units, wide), 0)
    unit_col = lax.broadcasted_iota(jnp.int32, (units, wide), 1)
    spread = (hadamard_sign(unit_row, unit_col // rows) * scale).astype(jnp.bfloat16)
    keep = lax.broadcasted_iota(jnp.int32, (tall, wide), 0) % rows == lax.broadcasted_iota(jnp.int32, (tall, wide), 1) % rows
    highs, lows = [], []
    for total in (sums[0] + side * sums[1], sums[0] - side * sums[1]):
        total = jnp.broadcast_to(total[:, None, :], (targets, rows, units)).reshape(tall, units)
        weights = jnp.dot(total.astype(jnp.bfloat16), spread, preferred_element_type=jnp.float32)
        high, low = two_parts(jnp.where(keep, weights, 0.0))
        highs.append(high)
        lows.append(low)
    left = jnp.concatenate(highs + highs + lows, axis=1)
    for step, low_z in itertools.product(range(near), range(low_count)):
        piece = (first_y + step) % near * low_count + low_z
        span = pl.ds(pl.multiple_of(piece * rows, rows), rows)
        parts = [two_parts(ref[:, span, :].reshape(wide, cols)) for ref in (own_ref, other_ref)]
        high = [part[0] for part in parts]
        low = [part[1] for part in parts]
        result = jnp.dot(left, jnp.concatenate(high + low + high, axis=0), preferred_element_type=jnp.float32)
        result = result.reshape(near, far, rows, cols)
        for turn in range(near):
            out_ref[jnp.where(core == 0, turn, step), jnp.where(core == 0, step, turn), low_z] = result[turn]


def mix(scale, place, meta, own, other, near, low_count, far):
    units, half, cols = own.shape
    rows = half // (near * low_count)
    vmem = pl.BlockSpec(memory_space=pltpu.VMEM)
    return pl.pallas_call(
        functools.partial(mix_kernel, scale),
        in_specs=[pl.BlockSpec(memory_space=pltpu.SMEM), vmem, vmem, vmem],
        out_specs=vmem,
        out_shape=jax.ShapeDtypeStruct((near, near, low_count, far, rows, cols), jnp.float32),
        compiler_params=pltpu.CompilerParams(vmem_limit_bytes=24 * MIB),
        cost_estimate=pl.CostEstimate(flops=2 * 3 * 128 * 512 * 256 * 8, bytes_accessed=5 * MIB, transcendentals=0),
        name="mix",
    )(place, meta, own, other)


Y, Z_LOW, Z_HIGH, X, CORE = 4, 2, 4, 4, 2


def flat_index(y, z_low, z_high, x, core):
    return (((y % Y * Z_LOW + z_low) * Z_HIGH + z_high) * X + x % X) * CORE + core


def places():
    return itertools.product(range(Y), range(Z_LOW), range(Z_HIGH), range(X), range(CORE))


def first_shift(value, step):
    pairs = []
    for y, z_low, z_high, x, core in places():
        to = (y, z_low, z_high, x + step, core) if core == 0 else (y + step, z_low, z_high, x, core)
        pairs.append((flat_index(y, z_low, z_high, x, core), flat_index(*to)))
    return lax.ppermute(value, AXES, pairs)


def second_groups():
    groups = []
    for core, fixed in itertools.product(range(CORE), range(X)):
        members = itertools.product(range(Y), range(Z_LOW), range(Z_HIGH))
        groups.append(
            [
                flat_index(free, z_low, z_high, fixed, core) if core == 0 else flat_index(fixed, z_low, z_high, free, core)
                for free, z_low, z_high in members
            ]
        )
    return groups


def body(matrix, row_signs, block_dest, block_signs):
    row_count, col_count = matrix.shape
    units = block_dest.shape[0]
    block = row_count // units
    groups = lax.axis_size("grp")
    devs = lax.axis_size("row")
    total_rows = row_count * devs * groups
    scale = math.sqrt(SKETCH / total_rows) / math.sqrt(row_count * devs)
    place = lax.axis_index(AXES).astype(jnp.int32).reshape(1)

    mine = jnp.stack([block_dest, block_signs])
    meta = lax.all_to_all(jnp.broadcast_to(mine[None], (devs, 2, units)), "row", 0, 0)
    matrix = matrix.reshape(units, block, col_count)
    row_signs = row_signs.reshape(units, block)
    own, send = transform(place, matrix, row_signs)
    other = lax.ppermute(send, "row", [(i, i ^ 1) for i in range(devs)])
    parts = mix(scale, place, meta, own, other, X, Z_LOW, Z_HIGH)

    got = {step: first_shift(parts[step], step) for step in (2, 1, 3)}
    part = (parts[0] + got[2]) + (got[1] + got[3])
    pieces = part.reshape(-1, 8, col_count)
    pieces = lax.all_to_all(pieces, AXES, 0, 0, axis_index_groups=second_groups())
    share = jnp.sum(pieces, axis=0)
    full = lax.all_to_all(jnp.broadcast_to(share[None], (groups, 8, col_count)), "grp", 0, 0)
    return full.reshape(groups * 8, col_count)


def solution(mesh):
    return jax.shard_map(
        body,
        mesh=mesh,
        in_specs=(P(AXES, None), P(AXES), P(AXES), P(AXES)),
        out_specs=P("row", None),
        check_vma=False,
    )
```

```python
import functools
import itertools
import math

import jax
import jax.numpy as jnp
from jax import lax
from jax.experimental import pallas as pl
from jax.experimental.pallas import tpu as pltpu
from jax.sharding import PartitionSpec as P

SKETCH = 2048
MIB = 1 << 20
AXES = ("grp", "row")


def parity(bits):
    for shift in (8, 4, 2, 1):
        bits = bits ^ bits >> shift
    return bits & 1


def hadamard_sign(rows, cols):
    return (1 - 2 * parity(rows & cols)).astype(jnp.float32)


def two_parts(value):
    high = value.astype(jnp.bfloat16)
    low = (value - high.astype(jnp.float32)).astype(jnp.bfloat16)
    return high, low


def transform_kernel(place_ref, matrix_hbm, signs_hbm, own_ref, send_ref, matrix_ref, signs_ref, sems, signs_sem):
    parts, step, block, _ = matrix_ref.shape
    half = block // 2
    signs_copy = pltpu.make_async_copy(signs_hbm, signs_ref, signs_sem)
    signs_copy.start()
    copies = [
        pltpu.make_async_copy(matrix_hbm.at[pl.ds(part * step, step)], matrix_ref.at[part], sems.at[part])
        for part in range(parts)
    ]
    for copy in copies:
        copy.start()
    core = place_ref[0] & 1
    out_row = lax.broadcasted_iota(jnp.int32, (block, block), 0)
    in_row = lax.broadcasted_iota(jnp.int32, (block, block), 1)
    hadamard = hadamard_sign(out_row ^ core * half, in_row)
    signs_copy.wait()
    for part in range(parts):
        copies[part].wait()
        for place in range(step):
            unit = part * step + place
            high, low = two_parts(matrix_ref[part, place])
            signed = (hadamard * signs_ref[pl.ds(unit, 1), :].astype(jnp.float32)).astype(jnp.bfloat16)
            result = jnp.dot(
                jnp.concatenate([signed, signed], axis=1),
                jnp.concatenate([high, low], axis=0),
                preferred_element_type=jnp.float32,
            )
            own_ref[unit] = result[:half]
            send_ref[unit] = result[half:]


def transform(place, matrix, row_signs):
    count, block, cols = matrix.shape
    parts = 8
    half = jax.ShapeDtypeStruct((count, block // 2, cols), jnp.float32)
    hbm = pl.BlockSpec(memory_space=pltpu.HBM)
    vmem = pl.BlockSpec(memory_space=pltpu.VMEM)
    return pl.pallas_call(
        transform_kernel,
        in_specs=[pl.BlockSpec(memory_space=pltpu.SMEM), hbm, hbm],
        out_specs=[vmem, vmem],
        out_shape=[half, half],
        scratch_shapes=[
            pltpu.VMEM((parts, count // parts, block, cols), jnp.float32),
            pltpu.VMEM((count, block), jnp.int32),
            pltpu.SemaphoreType.DMA((parts,)),
            pltpu.SemaphoreType.DMA,
        ],
        compiler_params=pltpu.CompilerParams(vmem_limit_bytes=16 * MIB),
        cost_estimate=pl.CostEstimate(flops=2 * 2 * 128 * 128 * 256 * 32, bytes_accessed=8 * MIB, transcendentals=0),
        name="transform",
    )(place, pltpu.with_memory_space_constraint(matrix, pltpu.HBM), pltpu.with_memory_space_constraint(row_signs, pltpu.HBM))


def mix_kernel(scale, place_ref, meta_ref, own_ref, other_ref, out_ref):
    near, _, low_count, far, rows, cols = out_ref.shape
    sources, _, units = meta_ref.shape
    targets = near * far
    me = place_ref[0] % sources
    core = me & 1
    first_x = jnp.where(core == 0, me >> 1, 0)
    first_y = jnp.where(core == 0, 0, place_ref[0] // sources // low_count)
    index = lax.broadcasted_iota(jnp.int32, (targets, units), 0)
    target = index % far * near + (index // far + first_x) % near
    sums = [jnp.zeros((targets, units), jnp.float32) for _ in range(2)]
    for source in range(sources):
        flip = 1 - 2 * parity((me >> 1) & (source >> 1))
        dests = meta_ref[source, 0:1, :]
        signs = meta_ref[source, 1:2, :] * flip
        routed = jnp.where(dests == target, signs.astype(jnp.float32), 0.0)
        sums[source & 1] = sums[source & 1] + routed
    side = (1 - 2 * core).astype(jnp.float32)
    tall, wide = targets * rows, units * rows
    unit_row = lax.broadcasted_iota(jnp.int32, (units, wide), 0)
    unit_col = lax.broadcasted_iota(jnp.int32, (units, wide), 1)
    spread = (hadamard_sign(unit_row, unit_col // rows) * scale).astype(jnp.bfloat16)
    keep = lax.broadcasted_iota(jnp.int32, (tall, wide), 0) % rows == lax.broadcasted_iota(jnp.int32, (tall, wide), 1) % rows
    highs, lows = [], []
    for total in (sums[0] + side * sums[1], sums[0] - side * sums[1]):
        total = jnp.broadcast_to(total[:, None, :], (targets, rows, units)).reshape(tall, units)
        weights = jnp.dot(total.astype(jnp.bfloat16), spread, preferred_element_type=jnp.float32)
        high, low = two_parts(jnp.where(keep, weights, 0.0))
        highs.append(high)
        lows.append(low)
    left = jnp.concatenate(highs, axis=1)
    stacked = jnp.concatenate([left, jnp.concatenate(lows, axis=1)], axis=0)
    for step, low_z in itertools.product(range(near), range(low_count)):
        piece = (first_y + step) % near * low_count + low_z
        span = pl.ds(pl.multiple_of(piece * rows, rows), rows)
        parts = [two_parts(ref[:, span, :].reshape(wide, cols)) for ref in (own_ref, other_ref)]
        high, low = (jnp.concatenate(each, axis=0) for each in zip(*parts))
        both = jnp.dot(stacked, high, preferred_element_type=jnp.float32)
        result = jnp.dot(left, low, preferred_element_type=jnp.float32) + (both[:tall] + both[tall:])
        result = result.reshape(near, far, rows, cols)
        for turn in range(near):
            out_ref[jnp.where(core == 0, turn, step), jnp.where(core == 0, step, turn), low_z] = result[turn]


def mix(scale, place, meta, own, other, near, low_count, far):
    units, half, cols = own.shape
    rows = half // (near * low_count)
    vmem = pl.BlockSpec(memory_space=pltpu.VMEM)
    return pl.pallas_call(
        functools.partial(mix_kernel, scale),
        in_specs=[pl.BlockSpec(memory_space=pltpu.SMEM), vmem, vmem, vmem],
        out_specs=vmem,
        out_shape=jax.ShapeDtypeStruct((near, near, low_count, far, rows, cols), jnp.float32),
        compiler_params=pltpu.CompilerParams(vmem_limit_bytes=24 * MIB),
        cost_estimate=pl.CostEstimate(flops=2 * 3 * 128 * 512 * 256 * 8, bytes_accessed=5 * MIB, transcendentals=0),
        name="mix",
    )(place, meta, own, other)


Y, Z_LOW, Z_HIGH, X, CORE = 4, 2, 4, 4, 2


def flat_index(y, z_low, z_high, x, core):
    return (((y % Y * Z_LOW + z_low) * Z_HIGH + z_high) * X + x % X) * CORE + core


def places():
    return itertools.product(range(Y), range(Z_LOW), range(Z_HIGH), range(X), range(CORE))


def first_shift(value, step):
    pairs = []
    for y, z_low, z_high, x, core in places():
        to = (y, z_low, z_high, x + step, core) if core == 0 else (y + step, z_low, z_high, x, core)
        pairs.append((flat_index(y, z_low, z_high, x, core), flat_index(*to)))
    return lax.ppermute(value, AXES, pairs)


def second_groups():
    groups = []
    for core, fixed in itertools.product(range(CORE), range(X)):
        members = itertools.product(range(Y), range(Z_LOW), range(Z_HIGH))
        groups.append(
            [
                flat_index(free, z_low, z_high, fixed, core) if core == 0 else flat_index(fixed, z_low, z_high, free, core)
                for free, z_low, z_high in members
            ]
        )
    return groups


def body(matrix, row_signs, block_dest, block_signs):
    row_count, col_count = matrix.shape
    units = block_dest.shape[0]
    block = row_count // units
    groups = lax.axis_size("grp")
    devs = lax.axis_size("row")
    total_rows = row_count * devs * groups
    scale = math.sqrt(SKETCH / total_rows) / math.sqrt(row_count * devs)
    place = lax.axis_index(AXES).astype(jnp.int32).reshape(1)

    mine = jnp.stack([block_dest, block_signs])
    meta = lax.all_to_all(jnp.broadcast_to(mine[None], (devs, 2, units)), "row", 0, 0)
    matrix = matrix.reshape(units, block, col_count)
    row_signs = row_signs.reshape(units, block)
    own, send = transform(place, matrix, row_signs)
    other = lax.ppermute(send, "row", [(i, i ^ 1) for i in range(devs)])
    parts = mix(scale, place, meta, own, other, X, Z_LOW, Z_HIGH)

    got = {step: first_shift(parts[step], step) for step in (2, 1, 3)}
    part = (parts[0] + got[2]) + (got[1] + got[3])
    pieces = part.reshape(-1, 8, col_count)
    pieces = lax.all_to_all(pieces, AXES, 0, 0, axis_index_groups=second_groups())
    share = jnp.sum(pieces, axis=0)
    full = lax.all_to_all(jnp.broadcast_to(share[None], (groups, 8, col_count)), "grp", 0, 0)
    return full.reshape(groups * 8, col_count)


def solution(mesh):
    return jax.shard_map(
        body,
        mesh=mesh,
        in_specs=(P(AXES, None), P(AXES), P(AXES), P(AXES)),
        out_specs=P("row", None),
        check_vma=False,
    )
```

```python
import functools
import itertools
import math

import jax
import jax.numpy as jnp
from jax import lax
from jax.experimental import pallas as pl
from jax.experimental.pallas import tpu as pltpu
from jax.sharding import PartitionSpec as P

SKETCH = 2048
MIB = 1 << 20
AXES = ("grp", "row")


def parity(bits):
    for shift in (8, 4, 2, 1):
        bits = bits ^ bits >> shift
    return bits & 1


def hadamard_sign(rows, cols):
    return (1 - 2 * parity(rows & cols)).astype(jnp.float32)


def two_parts(value):
    high = value.astype(jnp.bfloat16)
    low = (value - high.astype(jnp.float32)).astype(jnp.bfloat16)
    return high, low


def transform_kernel(place_ref, matrix_hbm, signs_hbm, own_ref, send_ref, matrix_ref, signs_ref, sems, signs_sem):
    parts, step, block, _ = matrix_ref.shape
    half = block // 2
    signs_copy = pltpu.make_async_copy(signs_hbm, signs_ref, signs_sem)
    signs_copy.start()
    copies = [
        pltpu.make_async_copy(matrix_hbm.at[pl.ds(part * step, step)], matrix_ref.at[part], sems.at[part])
        for part in range(parts)
    ]
    for copy in copies:
        copy.start()
    core = place_ref[0] & 1
    out_row = lax.broadcasted_iota(jnp.int32, (block, block), 0)
    in_row = lax.broadcasted_iota(jnp.int32, (block, block), 1)
    hadamard = hadamard_sign(out_row ^ core * half, in_row)
    signs_copy.wait()
    for part in range(parts):
        copies[part].wait()
        for place in range(step):
            unit = part * step + place
            high, low = two_parts(matrix_ref[part, place])
            signed = (hadamard * signs_ref[pl.ds(unit, 1), :].astype(jnp.float32)).astype(jnp.bfloat16)
            result = jnp.dot(
                jnp.concatenate([signed, signed], axis=1),
                jnp.concatenate([high, low], axis=0),
                preferred_element_type=jnp.float32,
            )
            own_ref[unit] = result[:half]
            send_ref[unit] = result[half:]


def transform(place, matrix, row_signs):
    count, block, cols = matrix.shape
    parts = 4
    half = jax.ShapeDtypeStruct((count, block // 2, cols), jnp.float32)
    hbm = pl.BlockSpec(memory_space=pltpu.HBM)
    vmem = pl.BlockSpec(memory_space=pltpu.VMEM)
    return pl.pallas_call(
        transform_kernel,
        in_specs=[pl.BlockSpec(memory_space=pltpu.SMEM), hbm, hbm],
        out_specs=[vmem, vmem],
        out_shape=[half, half],
        scratch_shapes=[
            pltpu.VMEM((parts, count // parts, block, cols), jnp.float32),
            pltpu.VMEM((count, block), jnp.int32),
            pltpu.SemaphoreType.DMA((parts,)),
            pltpu.SemaphoreType.DMA,
        ],
        compiler_params=pltpu.CompilerParams(vmem_limit_bytes=16 * MIB),
        cost_estimate=pl.CostEstimate(flops=2 * 2 * 128 * 128 * 256 * 32, bytes_accessed=8 * MIB, transcendentals=0),
        name="transform",
    )(place, pltpu.with_memory_space_constraint(matrix, pltpu.HBM), pltpu.with_memory_space_constraint(row_signs, pltpu.HBM))


def mix_kernel(scale, place_ref, meta_ref, own_ref, other_ref, out_ref):
    near, _, low_count, far, rows, cols = out_ref.shape
    sources, _, units = meta_ref.shape
    targets = near * far
    me = place_ref[0] % sources
    core = me & 1
    first_x = jnp.where(core == 0, me >> 1, 0)
    first_y = jnp.where(core == 0, 0, place_ref[0] // sources // low_count)
    index = lax.broadcasted_iota(jnp.int32, (targets, units), 0)
    target = index % far * near + (index // far + first_x) % near
    sums = [jnp.zeros((targets, units), jnp.float32) for _ in range(2)]
    for source in range(sources):
        flip = 1 - 2 * parity((me >> 1) & (source >> 1))
        dests = meta_ref[source, 0:1, :]
        signs = meta_ref[source, 1:2, :] * flip
        routed = jnp.where(dests == target, signs.astype(jnp.float32), 0.0)
        sums[source & 1] = sums[source & 1] + routed
    side = (1 - 2 * core).astype(jnp.float32)
    tall, wide = targets * rows, units * rows
    unit_row = lax.broadcasted_iota(jnp.int32, (units, wide), 0)
    unit_col = lax.broadcasted_iota(jnp.int32, (units, wide), 1)
    spread = (hadamard_sign(unit_row, unit_col // rows) * scale).astype(jnp.bfloat16)
    keep = lax.broadcasted_iota(jnp.int32, (tall, wide), 0) % rows == lax.broadcasted_iota(jnp.int32, (tall, wide), 1) % rows
    highs, lows = [], []
    for total in (sums[0] + side * sums[1], sums[0] - side * sums[1]):
        total = jnp.broadcast_to(total[:, None, :], (targets, rows, units)).reshape(tall, units)
        weights = jnp.dot(total.astype(jnp.bfloat16), spread, preferred_element_type=jnp.float32)
        high, low = two_parts(jnp.where(keep, weights, 0.0))
        highs.append(high)
        lows.append(low)
    left = jnp.concatenate(highs, axis=1)
    stacked = jnp.concatenate([left, jnp.concatenate(lows, axis=1)], axis=0)
    for step, low_z in itertools.product(range(near), range(low_count)):
        piece = (first_y + step) % near * low_count + low_z
        span = pl.ds(pl.multiple_of(piece * rows, rows), rows)
        parts = [two_parts(ref[:, span, :].reshape(wide, cols)) for ref in (own_ref, other_ref)]
        high, low = (jnp.concatenate(each, axis=0) for each in zip(*parts))
        both = jnp.dot(stacked, high, preferred_element_type=jnp.float32)
        result = jnp.dot(left, low, preferred_element_type=jnp.float32) + (both[:tall] + both[tall:])
        result = result.reshape(near, far, rows, cols)
        for turn in range(near):
            out_ref[jnp.where(core == 0, turn, step), jnp.where(core == 0, step, turn), low_z] = result[turn]


def mix(scale, place, meta, own, other, near, low_count, far):
    units, half, cols = own.shape
    rows = half // (near * low_count)
    vmem = pl.BlockSpec(memory_space=pltpu.VMEM)
    return pl.pallas_call(
        functools.partial(mix_kernel, scale),
        in_specs=[pl.BlockSpec(memory_space=pltpu.SMEM), vmem, vmem, vmem],
        out_specs=vmem,
        out_shape=jax.ShapeDtypeStruct((near, near, low_count, far, rows, cols), jnp.float32),
        compiler_params=pltpu.CompilerParams(vmem_limit_bytes=24 * MIB),
        cost_estimate=pl.CostEstimate(flops=2 * 3 * 128 * 512 * 256 * 8, bytes_accessed=5 * MIB, transcendentals=0),
        name="mix",
    )(place, meta, own, other)


Y, Z_LOW, Z_HIGH, X, CORE = 4, 2, 4, 4, 2


def flat_index(y, z_low, z_high, x, core):
    return (((y % Y * Z_LOW + z_low) * Z_HIGH + z_high) * X + x % X) * CORE + core


def places():
    return itertools.product(range(Y), range(Z_LOW), range(Z_HIGH), range(X), range(CORE))


def first_shift(value, step):
    pairs = []
    for y, z_low, z_high, x, core in places():
        to = (y, z_low, z_high, x + step, core) if core == 0 else (y + step, z_low, z_high, x, core)
        pairs.append((flat_index(y, z_low, z_high, x, core), flat_index(*to)))
    return lax.ppermute(value, AXES, pairs)


def second_groups():
    groups = []
    for core, fixed in itertools.product(range(CORE), range(X)):
        members = itertools.product(range(Y), range(Z_LOW), range(Z_HIGH))
        groups.append(
            [
                flat_index(free, z_low, z_high, fixed, core) if core == 0 else flat_index(fixed, z_low, z_high, free, core)
                for free, z_low, z_high in members
            ]
        )
    return groups


def body(matrix, row_signs, block_dest, block_signs):
    row_count, col_count = matrix.shape
    units = block_dest.shape[0]
    block = row_count // units
    groups = lax.axis_size("grp")
    devs = lax.axis_size("row")
    total_rows = row_count * devs * groups
    scale = math.sqrt(SKETCH / total_rows) / math.sqrt(row_count * devs)
    place = lax.axis_index(AXES).astype(jnp.int32).reshape(1)

    mine = jnp.stack([block_dest, block_signs])
    meta = lax.all_to_all(jnp.broadcast_to(mine[None], (devs, 2, units)), "row", 0, 0)
    matrix = matrix.reshape(units, block, col_count)
    row_signs = row_signs.reshape(units, block)
    own, send = transform(place, matrix, row_signs)
    other = lax.ppermute(send, "row", [(i, i ^ 1) for i in range(devs)])
    parts = mix(scale, place, meta, own, other, X, Z_LOW, Z_HIGH)

    got = {step: first_shift(parts[step], step) for step in (2, 1, 3)}
    part = (parts[0] + got[2]) + (got[1] + got[3])
    pieces = part.reshape(-1, 8, col_count)
    pieces = lax.all_to_all(pieces, AXES, 0, 0, axis_index_groups=second_groups())
    share = jnp.sum(pieces, axis=0)
    full = lax.all_to_all(jnp.broadcast_to(share[None], (groups, 8, col_count)), "grp", 0, 0)
    return full.reshape(groups * 8, col_count)


def solution(mesh):
    return jax.shard_map(
        body,
        mesh=mesh,
        in_specs=(P(AXES, None), P(AXES), P(AXES), P(AXES)),
        out_specs=P("row", None),
        check_vma=False,
    )
```

```python
import functools
import itertools
import math

import jax
import jax.numpy as jnp
from jax import lax
from jax.experimental import pallas as pl
from jax.experimental.pallas import tpu as pltpu
from jax.sharding import PartitionSpec as P

SKETCH = 2048
MIB = 1 << 20
AXES = ("grp", "row")


def parity(bits):
    for shift in (8, 4, 2, 1):
        bits = bits ^ bits >> shift
    return bits & 1


def hadamard_sign(rows, cols):
    return (1 - 2 * parity(rows & cols)).astype(jnp.float32)


def two_parts(value):
    high = value.astype(jnp.bfloat16)
    low = (value - high.astype(jnp.float32)).astype(jnp.bfloat16)
    return high, low


def transform_kernel(cuts, place_ref, matrix_hbm, signs_hbm, own_ref, send_ref, matrix_ref, signs_ref, sems, signs_sem):
    block = matrix_ref.shape[1]
    half = block // 2
    signs_copy = pltpu.make_async_copy(signs_hbm, signs_ref, signs_sem)
    signs_copy.start()
    copies = []
    for part, (first, last) in enumerate(itertools.pairwise(cuts)):
        span = pl.ds(first, last - first)
        copies.append(pltpu.make_async_copy(matrix_hbm.at[span], matrix_ref.at[span], sems.at[part]))
        copies[-1].start()
    core = place_ref[0] & 1
    out_row = lax.broadcasted_iota(jnp.int32, (block, block), 0)
    in_row = lax.broadcasted_iota(jnp.int32, (block, block), 1)
    hadamard = hadamard_sign(out_row ^ core * half, in_row).astype(jnp.bfloat16)
    signs_copy.wait()
    for copy, (first, last) in zip(copies, itertools.pairwise(cuts)):
        copy.wait()
        for unit in range(first, last):
            high, low = two_parts(matrix_ref[unit])
            signed = hadamard * signs_ref[pl.ds(unit, 1), :].astype(jnp.float32).astype(jnp.bfloat16)
            result = jnp.dot(
                jnp.concatenate([signed, signed], axis=1),
                jnp.concatenate([high, low], axis=0),
                preferred_element_type=jnp.float32,
            )
            own_ref[unit] = result[:half]
            send_ref[unit] = result[half:]


def transform(place, matrix, row_signs):
    count, block, cols = matrix.shape
    cuts = (0, count // 4, count * 5 // 8, count)
    half = jax.ShapeDtypeStruct((count, block // 2, cols), jnp.float32)
    hbm = pl.BlockSpec(memory_space=pltpu.HBM)
    vmem = pl.BlockSpec(memory_space=pltpu.VMEM)
    return pl.pallas_call(
        functools.partial(transform_kernel, cuts),
        in_specs=[pl.BlockSpec(memory_space=pltpu.SMEM), hbm, hbm],
        out_specs=[vmem, vmem],
        out_shape=[half, half],
        scratch_shapes=[
            pltpu.VMEM(matrix.shape, jnp.float32),
            pltpu.VMEM((count, block), jnp.int32),
            pltpu.SemaphoreType.DMA((len(cuts) - 1,)),
            pltpu.SemaphoreType.DMA,
        ],
        compiler_params=pltpu.CompilerParams(vmem_limit_bytes=16 * MIB),
        cost_estimate=pl.CostEstimate(flops=2 * 2 * 128 * 128 * 256 * 32, bytes_accessed=8 * MIB, transcendentals=0),
        name="transform",
    )(
        place,
        pltpu.with_memory_space_constraint(matrix, pltpu.HBM),
        pltpu.with_memory_space_constraint(row_signs, pltpu.HBM),
    )


def mix_kernel(scale, place_ref, meta_ref, own_ref, other_ref, out_ref):
    near, _, low_count, far, rows, cols = out_ref.shape
    sources, _, units = meta_ref.shape
    targets = near * far
    me = place_ref[0] % sources
    core = me & 1
    first_x = jnp.where(core == 0, me >> 1, 0)
    first_y = jnp.where(core == 0, 0, place_ref[0] // sources // low_count)
    index = lax.broadcasted_iota(jnp.int32, (targets, units), 0)
    target = index % far * near + (index // far + first_x) % near
    sums = [jnp.zeros((targets, units), jnp.float32) for _ in range(2)]
    for source in range(sources):
        flip = 1 - 2 * parity((me >> 1) & (source >> 1))
        dests = meta_ref[source, 0:1, :]
        signs = meta_ref[source, 1:2, :] * flip
        routed = jnp.where(dests == target, signs.astype(jnp.float32), 0.0)
        sums[source & 1] = sums[source & 1] + routed
    side = (1 - 2 * core).astype(jnp.float32)
    tall, wide = targets * rows, units * rows
    unit_row = lax.broadcasted_iota(jnp.int32, (units, wide), 0)
    unit_col = lax.broadcasted_iota(jnp.int32, (units, wide), 1)
    spread = (hadamard_sign(unit_row, unit_col // rows) * scale).astype(jnp.bfloat16)
    keep = lax.broadcasted_iota(jnp.int32, (tall, wide), 0) % rows == lax.broadcasted_iota(jnp.int32, (tall, wide), 1) % rows
    highs, lows = [], []
    for total in (sums[0] + side * sums[1], sums[0] - side * sums[1]):
        total = jnp.broadcast_to(total[:, None, :], (targets, rows, units)).reshape(tall, units)
        weights = jnp.dot(total.astype(jnp.bfloat16), spread, preferred_element_type=jnp.float32)
        high, low = two_parts(jnp.where(keep, weights, 0.0))
        highs.append(high)
        lows.append(low)
    left = jnp.concatenate(highs, axis=1)
    stacked = jnp.concatenate([left, jnp.concatenate(lows, axis=1)], axis=0)
    for step, low_z in itertools.product(range(near), range(low_count)):
        piece = (first_y + step) % near * low_count + low_z
        span = pl.ds(pl.multiple_of(piece * rows, rows), rows)
        parts = [two_parts(ref[:, span, :].reshape(wide, cols)) for ref in (own_ref, other_ref)]
        high, low = (jnp.concatenate(each, axis=0) for each in zip(*parts))
        both = jnp.dot(stacked, high, preferred_element_type=jnp.float32)
        result = jnp.dot(left, low, preferred_element_type=jnp.float32) + (both[:tall] + both[tall:])
        result = result.reshape(near, far, rows, cols)
        for turn in range(near):
            out_ref[jnp.where(core == 0, turn, step), jnp.where(core == 0, step, turn), low_z] = result[turn]


def mix(scale, place, meta, own, other, near, low_count, far):
    units, half, cols = own.shape
    rows = half // (near * low_count)
    vmem = pl.BlockSpec(memory_space=pltpu.VMEM)
    return pl.pallas_call(
        functools.partial(mix_kernel, scale),
        in_specs=[pl.BlockSpec(memory_space=pltpu.SMEM), vmem, vmem, vmem],
        out_specs=vmem,
        out_shape=jax.ShapeDtypeStruct((near, near, low_count, far, rows, cols), jnp.float32),
        compiler_params=pltpu.CompilerParams(vmem_limit_bytes=24 * MIB),
        cost_estimate=pl.CostEstimate(flops=2 * 3 * 128 * 512 * 256 * 8, bytes_accessed=5 * MIB, transcendentals=0),
        name="mix",
    )(place, meta, own, other)


Y, Z_LOW, Z_HIGH, X, CORE = 4, 2, 4, 4, 2


def flat_index(y, z_low, z_high, x, core):
    return (((y % Y * Z_LOW + z_low) * Z_HIGH + z_high) * X + x % X) * CORE + core


def places():
    return itertools.product(range(Y), range(Z_LOW), range(Z_HIGH), range(X), range(CORE))


def first_shift(value, step):
    pairs = []
    for y, z_low, z_high, x, core in places():
        to = (y, z_low, z_high, x + step, core) if core == 0 else (y + step, z_low, z_high, x, core)
        pairs.append((flat_index(y, z_low, z_high, x, core), flat_index(*to)))
    return lax.ppermute(value, AXES, pairs)


def second_groups():
    groups = []
    for core, fixed in itertools.product(range(CORE), range(X)):
        members = itertools.product(range(Y), range(Z_LOW), range(Z_HIGH))
        groups.append(
            [
                flat_index(free, z_low, z_high, fixed, core) if core == 0 else flat_index(fixed, z_low, z_high, free, core)
                for free, z_low, z_high in members
            ]
        )
    return groups


def body(matrix, row_signs, block_dest, block_signs):
    row_count, col_count = matrix.shape
    units = block_dest.shape[0]
    block = row_count // units
    groups = lax.axis_size("grp")
    devs = lax.axis_size("row")
    total_rows = row_count * devs * groups
    scale = math.sqrt(SKETCH / total_rows) / math.sqrt(row_count * devs)
    place = lax.axis_index(AXES).astype(jnp.int32).reshape(1)

    mine = jnp.stack([block_dest, block_signs])
    meta = lax.all_to_all(jnp.broadcast_to(mine[None], (devs, 2, units)), "row", 0, 0)
    matrix = matrix.reshape(units, block, col_count)
    row_signs = row_signs.reshape(units, block)
    own, send = transform(place, matrix, row_signs)
    other = lax.ppermute(send, "row", [(i, i ^ 1) for i in range(devs)])
    parts = mix(scale, place, meta, own, other, X, Z_LOW, Z_HIGH)

    got = {step: first_shift(parts[step], step) for step in (2, 1, 3)}
    part = (parts[0] + got[2]) + (got[1] + got[3])
    pieces = part.reshape(-1, 8, col_count)
    pieces = lax.all_to_all(pieces, AXES, 0, 0, axis_index_groups=second_groups())
    share = jnp.sum(pieces, axis=0)
    full = lax.all_to_all(jnp.broadcast_to(share[None], (groups, 8, col_count)), "grp", 0, 0)
    return full.reshape(groups * 8, col_count)


def solution(mesh):
    return jax.shard_map(
        body,
        mesh=mesh,
        in_specs=(P(AXES, None), P(AXES), P(AXES), P(AXES)),
        out_specs=P("row", None),
        check_vma=False,
    )
```

```python
import functools
import itertools
import math

import jax
import jax.numpy as jnp
from jax import lax
from jax.experimental import pallas as pl
from jax.experimental.pallas import tpu as pltpu
from jax.sharding import PartitionSpec as P

SKETCH = 2048
MIB = 1 << 20
AXES = ("grp", "row")


def parity(bits):
    for shift in (8, 4, 2, 1):
        bits = bits ^ bits >> shift
    return bits & 1


def hadamard_sign(rows, cols):
    return (1 - 2 * parity(rows & cols)).astype(jnp.float32)


def two_parts(value):
    high = value.astype(jnp.bfloat16)
    low = (value - high.astype(jnp.float32)).astype(jnp.bfloat16)
    return high, low


def mix_kernel(
    scale, place_ref, meta_ref, matrix_hbm, signs_hbm, other_hbm, other_signs_ref, out_ref, rows_ref, factor_ref, signs_ref, sems, signs_sem
):
    near, _, low_count, far, rows, cols = out_ref.shape
    sources, _, units = meta_ref.shape
    half = rows_ref.shape[2]
    targets = near * far
    me = place_ref[0] % sources
    core = me & 1
    first_row = pl.multiple_of(core * half, half)
    signs_copy = pltpu.make_async_copy(signs_hbm, signs_ref, signs_sem)
    signs_copy.start()
    first_x = jnp.where(core == 0, me >> 1, 0)
    first_y = jnp.where(core == 0, 0, place_ref[0] // sources // low_count)
    copies = []
    for step in range(near):
        first = pl.multiple_of((first_y + step) % near * low_count * rows, low_count * rows)
        for turn, ref in enumerate((matrix_hbm, other_hbm)):
            copies.append(
                pltpu.make_async_copy(
                    ref.at[:, pl.ds(pl.multiple_of(first_row + first, low_count * rows), low_count * rows), :],
                    rows_ref.at[turn, :, pl.ds(first, low_count * rows), :],
                    sems.at[step, turn],
                )
            )
            copies[-1].start()
    index = lax.broadcasted_iota(jnp.int32, (targets, units), 0)
    target = index % far * near + (index // far + first_x) % near
    sums = [jnp.zeros((targets, units), jnp.float32) for _ in range(2)]
    for source in range(sources):
        flip = 1 - 2 * parity((me >> 1) & (source >> 1))
        dests = meta_ref[source, 0:1, :]
        signs = meta_ref[source, 1:2, :] * flip
        routed = jnp.where(dests == target, signs.astype(jnp.float32), 0.0)
        sums[source & 1] = sums[source & 1] + routed
    side = (1 - 2 * core).astype(jnp.float32)
    tall, wide = targets * rows, units * rows
    unit_row = lax.broadcasted_iota(jnp.int32, (units, wide), 0)
    unit_col = lax.broadcasted_iota(jnp.int32, (units, wide), 1) // rows
    spread = (hadamard_sign(unit_row, unit_col) * scale).astype(jnp.bfloat16)
    repeat = (unit_row == unit_col).astype(jnp.bfloat16)
    keep = lax.broadcasted_iota(jnp.int32, (tall, wide), 0) % rows == lax.broadcasted_iota(jnp.int32, (tall, wide), 1) % rows
    signs_copy.wait()
    highs, lows = [], []
    for turn, (total, ref) in enumerate(
        ((sums[0] + side * sums[1], signs_ref), (sums[0] - side * sums[1], other_signs_ref))
    ):
        total = jnp.broadcast_to(total[:, None, :], (targets, rows, units)).reshape(tall, units)
        weights = jnp.dot(total.astype(jnp.bfloat16), spread, preferred_element_type=jnp.float32)
        high, low = two_parts(jnp.where(keep, weights, 0.0))
        highs.append(high)
        lows.append(low)
        factor_ref[:, pl.ds(turn * wide, wide)] = lax.dot_general(
            ref[...].astype(jnp.float32).astype(jnp.bfloat16),
            repeat,
            (((0,), (0,)), ((), ())),
            preferred_element_type=jnp.float32,
        )
    stacked = jnp.concatenate([jnp.concatenate(highs, axis=1), jnp.concatenate(lows, axis=1)], axis=0)
    for step, low_z in itertools.product(range(near), range(low_count)):
        if low_z == 0 and step % 2 == 0:
            for copy in copies[2 * step : 2 * step + 4]:
                copy.wait()
        piece = (first_y + step) % near * low_count + low_z
        span = pl.ds(pl.multiple_of(piece * rows, rows), rows)
        far_span = pl.ds(pl.multiple_of(first_row + piece * rows, rows), rows)
        factor = factor_ref[far_span, :]
        factor = jnp.concatenate([factor, factor], axis=0).astype(jnp.bfloat16)
        left = (stacked.reshape(tall // rows, 2 * rows, 2 * wide) * factor[None]).reshape(2 * tall, 2 * wide)
        parts = [two_parts(rows_ref[turn, :, span, :].reshape(wide, cols)) for turn in range(2)]
        high, low = (jnp.concatenate(each, axis=0) for each in zip(*parts))
        both = jnp.dot(left, high, preferred_element_type=jnp.float32)
        result = jnp.dot(left[:tall], low, preferred_element_type=jnp.float32) + (both[:tall] + both[tall:])
        result = result.reshape(near, far, rows, cols)
        for turn in range(near):
            out_ref[jnp.where(core == 0, turn, step), jnp.where(core == 0, step, turn), low_z] = result[turn]


def mix(scale, place, meta, matrix, signs, other, other_signs, near, low_count, far):
    units, block, cols = matrix.shape
    half = block // 2
    rows = half // (near * low_count)
    hbm = pl.BlockSpec(memory_space=pltpu.HBM)
    vmem = pl.BlockSpec(memory_space=pltpu.VMEM)
    return pl.pallas_call(
        functools.partial(mix_kernel, scale),
        in_specs=[pl.BlockSpec(memory_space=pltpu.SMEM), vmem, hbm, hbm, hbm, vmem],
        out_specs=vmem,
        out_shape=jax.ShapeDtypeStruct((near, near, low_count, far, rows, cols), jnp.float32),
        scratch_shapes=[
            pltpu.VMEM((2, units, half, cols), jnp.float32),
            pltpu.VMEM((block, 2 * units * rows), jnp.float32),
            pltpu.VMEM(signs.shape, jnp.int32),
            pltpu.SemaphoreType.DMA((near, 2)),
            pltpu.SemaphoreType.DMA,
        ],
        compiler_params=pltpu.CompilerParams(vmem_limit_bytes=24 * MIB),
        cost_estimate=pl.CostEstimate(flops=2 * 3 * 128 * 512 * 256 * 8, bytes_accessed=5 * MIB, transcendentals=0),
        name="mix",
    )(place, meta, *(pltpu.with_memory_space_constraint(value, pltpu.HBM) for value in (matrix, signs, other)), other_signs)


def finish_kernel(place_ref, mixed_ref, out_ref):
    block = mixed_ref.shape[0]
    half = block // 2
    row = lax.broadcasted_iota(jnp.int32, (half, block), 0) + (place_ref[0] & 1) * half
    hadamard = hadamard_sign(row, lax.broadcasted_iota(jnp.int32, (half, block), 1)).astype(jnp.bfloat16)
    value = mixed_ref[...]
    high = value.astype(jnp.bfloat16)
    middle, low = two_parts(value - high.astype(jnp.float32))
    out_ref[...] = jnp.dot(
        jnp.concatenate([hadamard] * 3, axis=1),
        jnp.concatenate([high, middle, low], axis=0),
        preferred_element_type=jnp.float32,
    )


def finish(place, mixed):
    vmem = pl.BlockSpec(memory_space=pltpu.VMEM)
    return pl.pallas_call(
        finish_kernel,
        in_specs=[pl.BlockSpec(memory_space=pltpu.SMEM), vmem],
        out_specs=vmem,
        out_shape=jax.ShapeDtypeStruct((mixed.shape[0] // 2, mixed.shape[1]), jnp.float32),
        compiler_params=pltpu.CompilerParams(vmem_limit_bytes=8 * MIB),
        name="finish",
    )(place, mixed)


Y, Z_LOW, Z_HIGH, X, CORE = 4, 2, 4, 4, 2


def flat_index(y, z_low, z_high, x, core):
    return (((y % Y * Z_LOW + z_low) * Z_HIGH + z_high) * X + x % X) * CORE + core


def places():
    return itertools.product(range(Y), range(Z_LOW), range(Z_HIGH), range(X), range(CORE))


def first_shift(value, step):
    pairs = []
    for y, z_low, z_high, x, core in places():
        to = (y, z_low, z_high, x + step, core) if core == 0 else (y + step, z_low, z_high, x, core)
        pairs.append((flat_index(y, z_low, z_high, x, core), flat_index(*to)))
    return lax.ppermute(value, AXES, pairs)


def second_groups():
    groups = []
    for core, fixed in itertools.product(range(CORE), range(X)):
        members = itertools.product(range(Y), range(Z_LOW), range(Z_HIGH))
        groups.append(
            [
                flat_index(free, z_low, z_high, fixed, core) if core == 0 else flat_index(fixed, z_low, z_high, free, core)
                for free, z_low, z_high in members
            ]
        )
    return groups


def last_groups():
    return [
        [flat_index(y, z_low, z_high, x, core) for core in range(CORE) for y in range(Y) for z_low in range(Z_LOW)]
        for z_high in range(Z_HIGH)
        for x in range(X)
    ]


def body(matrix, row_signs, block_dest, block_signs):
    row_count, col_count = matrix.shape
    units = block_dest.shape[0]
    block = row_count // units
    groups = lax.axis_size("grp")
    devs = lax.axis_size("row")
    total_rows = row_count * devs * groups
    scale = math.sqrt(SKETCH / total_rows) / math.sqrt(row_count * devs)
    place = lax.axis_index(AXES).astype(jnp.int32).reshape(1)

    mine, place = lax.optimization_barrier((jnp.stack([block_dest, block_signs]), place))
    meta = lax.all_to_all(jnp.broadcast_to(mine[None], (devs, 2, units)), "row", 0, 0)
    matrix = matrix.reshape(units, block, col_count)
    row_signs = row_signs.reshape(units, block)
    other, other_signs = (lax.ppermute(value, "row", [(i, i ^ 1) for i in range(devs)]) for value in (matrix, row_signs))
    parts = mix(scale, place, meta, matrix, row_signs, other, other_signs, X, Z_LOW, Z_HIGH)

    got = {step: first_shift(parts[step], step) for step in (2, 1, 3)}
    part = (parts[0] + got[2]) + (got[1] + got[3])
    pieces = part.reshape(-1, 8, col_count)
    pieces = lax.all_to_all(pieces, AXES, 0, 0, axis_index_groups=second_groups())
    share = jnp.sum(pieces, axis=0)
    full = jnp.broadcast_to(share[None], (CORE * groups, *share.shape))
    full = lax.all_to_all(full, AXES, 0, 0, axis_index_groups=last_groups())
    return finish(place, full.reshape(block, col_count))


def solution(mesh):
    return jax.shard_map(
        body,
        mesh=mesh,
        in_specs=(P(AXES, None), P(AXES), P(AXES), P(AXES)),
        out_specs=P("row", None),
        check_vma=False,
    )
```

```python
import functools
import itertools
import math

import jax
import jax.numpy as jnp
from jax import lax
from jax.experimental import pallas as pl
from jax.experimental.pallas import tpu as pltpu
from jax.sharding import PartitionSpec as P

SKETCH = 2048
MIB = 1 << 20
LANES = 128
AXES = ("grp", "row")


def parity(bits):
    for shift in (8, 4, 2, 1):
        bits = bits ^ bits >> shift
    return bits & 1


def hadamard_sign(rows, cols):
    return (1 - 2 * parity(rows & cols)).astype(jnp.float32)


def two_parts(value):
    high = value.astype(jnp.bfloat16)
    low = (value - high.astype(jnp.float32)).astype(jnp.bfloat16)
    return high, low


def transform_kernel(cuts, place_ref, matrix_hbm, signs_hbm, own_ref, send_ref, matrix_ref, signs_ref, sems, signs_sem):
    block = matrix_ref.shape[1]
    half = block // 2
    signs_copy = pltpu.make_async_copy(signs_hbm, signs_ref, signs_sem)
    signs_copy.start()
    copies = []
    for part, (first, last) in enumerate(itertools.pairwise(cuts)):
        span = pl.ds(first, last - first)
        copies.append(pltpu.make_async_copy(matrix_hbm.at[span], matrix_ref.at[span], sems.at[part]))
        copies[-1].start()
    core = place_ref[0] & 1
    out_row = lax.broadcasted_iota(jnp.int32, (block, block), 0)
    in_row = lax.broadcasted_iota(jnp.int32, (block, block), 1)
    hadamard = hadamard_sign(out_row ^ core * half, in_row).astype(jnp.bfloat16)
    signs_copy.wait()
    for copy, (first, last) in zip(copies, itertools.pairwise(cuts)):
        copy.wait()
        for unit in range(first, last):
            high, low = two_parts(matrix_ref[unit])
            signed = hadamard * signs_ref[pl.ds(unit, 1), :].astype(jnp.float32).astype(jnp.bfloat16)
            result = jnp.dot(
                jnp.concatenate([signed, signed], axis=1),
                jnp.concatenate([high, low], axis=0),
                preferred_element_type=jnp.float32,
            )
            own_ref[unit] = result[:half]
            send_ref[unit] = result[half:]


def transform(place, matrix, row_signs):
    count, block, cols = matrix.shape
    cuts = (0, count // 4, count * 5 // 8, count)
    half = jax.ShapeDtypeStruct((count, block // 2, cols), jnp.float32)
    hbm = pl.BlockSpec(memory_space=pltpu.HBM)
    vmem = pl.BlockSpec(memory_space=pltpu.VMEM)
    return pl.pallas_call(
        functools.partial(transform_kernel, cuts),
        in_specs=[pl.BlockSpec(memory_space=pltpu.SMEM), hbm, hbm],
        out_specs=[vmem, vmem],
        out_shape=[half, half],
        scratch_shapes=[
            pltpu.VMEM(matrix.shape, jnp.float32),
            pltpu.VMEM((count, block), jnp.int32),
            pltpu.SemaphoreType.DMA((len(cuts) - 1,)),
            pltpu.SemaphoreType.DMA,
        ],
        compiler_params=pltpu.CompilerParams(vmem_limit_bytes=16 * MIB),
        cost_estimate=pl.CostEstimate(flops=2 * 2 * 128 * 128 * 256 * 32, bytes_accessed=8 * MIB, transcendentals=0),
        name="transform",
    )(
        place,
        pltpu.with_memory_space_constraint(matrix, pltpu.HBM),
        pltpu.with_memory_space_constraint(row_signs, pltpu.HBM),
    )


def mix_kernel(scale, place_ref, meta_ref, own_ref, other_ref, out_ref):
    near, _, low_count, far, rows, cols = out_ref.shape
    chips = meta_ref.shape[0]
    units = own_ref.shape[0]
    sources = 2 * chips
    targets = near * far
    me = place_ref[0] % sources
    core = me & 1
    first_x = jnp.where(core == 0, me >> 1, 0)
    first_y = jnp.where(core == 0, 0, place_ref[0] // sources // low_count)
    index = lax.broadcasted_iota(jnp.int32, (targets, units), 0)
    target = index % far * near + (index // far + first_x) % near
    same, different = (jnp.zeros((targets, units), jnp.float32) for _ in range(2))
    for source in range(chips):
        flip = 1 - 2 * parity((me >> 1) & source)
        dests, signs, other_dests, other_signs = (meta_ref[source, row : row + 1, :units] for row in range(4))
        same = same + jnp.where(dests == target, (signs * flip).astype(jnp.float32), 0.0)
        different = different + jnp.where(other_dests == target, (other_signs * flip).astype(jnp.float32), 0.0)
    side = (1 - 2 * core).astype(jnp.float32)
    tall, wide = targets * rows, units * rows
    unit_row = lax.broadcasted_iota(jnp.int32, (units, wide), 0)
    unit_col = lax.broadcasted_iota(jnp.int32, (units, wide), 1)
    spread = (hadamard_sign(unit_row, unit_col // rows) * scale).astype(jnp.bfloat16)
    keep = lax.broadcasted_iota(jnp.int32, (tall, wide), 0) % rows == lax.broadcasted_iota(jnp.int32, (tall, wide), 1) % rows
    highs, lows = [], []
    for total in (side * same + different, same - side * different):
        total = jnp.broadcast_to(total[:, None, :], (targets, rows, units)).reshape(tall, units)
        weights = jnp.dot(total.astype(jnp.bfloat16), spread, preferred_element_type=jnp.float32)
        high, low = two_parts(jnp.where(keep, weights, 0.0))
        highs.append(high)
        lows.append(low)
    left = jnp.concatenate(highs, axis=1)
    stacked = jnp.concatenate([left, jnp.concatenate(lows, axis=1)], axis=0)
    for step, low_z in itertools.product(range(near), range(low_count)):
        piece = (first_y + step) % near * low_count + low_z
        span = pl.ds(pl.multiple_of(piece * rows, rows), rows)
        parts = [two_parts(ref[:, span, :].reshape(wide, cols)) for ref in (own_ref, other_ref)]
        high, low = (jnp.concatenate(each, axis=0) for each in zip(*parts))
        both = jnp.dot(stacked, high, preferred_element_type=jnp.float32)
        result = jnp.dot(left, low, preferred_element_type=jnp.float32) + (both[:tall] + both[tall:])
        result = result.reshape(near, far, rows, cols)
        for turn in range(near):
            out_ref[jnp.where(core == 0, turn, step), jnp.where(core == 0, step, turn), low_z] = result[turn]


def mix(scale, place, meta, own, other, near, low_count, far):
    units, half, cols = own.shape
    rows = half // (near * low_count)
    vmem = pl.BlockSpec(memory_space=pltpu.VMEM)
    return pl.pallas_call(
        functools.partial(mix_kernel, scale),
        in_specs=[pl.BlockSpec(memory_space=pltpu.SMEM), vmem, vmem, vmem],
        out_specs=vmem,
        out_shape=jax.ShapeDtypeStruct((near, near, low_count, far, rows, cols), jnp.float32),
        compiler_params=pltpu.CompilerParams(vmem_limit_bytes=24 * MIB),
        cost_estimate=pl.CostEstimate(flops=2 * 3 * 128 * 512 * 256 * 8, bytes_accessed=5 * MIB, transcendentals=0),
        name="mix",
    )(place, meta, own, other)


Y, Z_LOW, Z_HIGH, X, CORE = 4, 2, 4, 4, 2


def flat_index(y, z_low, z_high, x, core):
    return (((y % Y * Z_LOW + z_low) * Z_HIGH + z_high) * X + x % X) * CORE + core


def places():
    return itertools.product(range(Y), range(Z_LOW), range(Z_HIGH), range(X), range(CORE))


def first_shift(value, step):
    pairs = []
    for y, z_low, z_high, x, core in places():
        to = (y, z_low, z_high, x + step, core) if core == 0 else (y + step, z_low, z_high, x, core)
        pairs.append((flat_index(y, z_low, z_high, x, core), flat_index(*to)))
    return lax.ppermute(value, AXES, pairs)


def second_groups():
    groups = []
    for core, fixed in itertools.product(range(CORE), range(X)):
        members = itertools.product(range(Y), range(Z_LOW), range(Z_HIGH))
        groups.append(
            [
                flat_index(free, z_low, z_high, fixed, core) if core == 0 else flat_index(fixed, z_low, z_high, free, core)
                for free, z_low, z_high in members
            ]
        )
    return groups


def body(matrix, row_signs, block_dest, block_signs):
    row_count, col_count = matrix.shape
    units = block_dest.shape[0]
    block = row_count // units
    groups = lax.axis_size("grp")
    devs = lax.axis_size("row")
    total_rows = row_count * devs * groups
    scale = math.sqrt(SKETCH / total_rows) / math.sqrt(row_count * devs)
    place = lax.axis_index(AXES).astype(jnp.int32).reshape(1)

    cores = [(i, i ^ 1) for i in range(devs)]
    mine = jnp.stack([block_dest, block_signs])
    mine = jnp.concatenate([mine, lax.ppermute(mine, "row", cores)])
    mine = jnp.pad(mine, ((0, 0), (0, LANES - units)))
    same_core = [list(range(core, devs, CORE)) for core in range(CORE)]
    matrix = matrix.reshape(units, block, col_count)
    own, send = transform(place, matrix, row_signs.reshape(units, block))
    send, mine = lax.optimization_barrier((send, mine))
    other = lax.ppermute(send, "row", cores)
    meta = jnp.broadcast_to(mine[None], (devs // CORE, *mine.shape))
    meta = lax.all_to_all(meta, "row", 0, 0, axis_index_groups=same_core)
    parts = mix(scale, place, meta, own, other, X, Z_LOW, Z_HIGH)

    got = {step: first_shift(parts[step], step) for step in (2, 1, 3)}
    part = (parts[0] + got[2]) + (got[1] + got[3])
    pieces = part.reshape(-1, 8, col_count)
    pieces = lax.all_to_all(pieces, AXES, 0, 0, axis_index_groups=second_groups())
    share = jnp.sum(pieces, axis=0)
    full = lax.all_to_all(jnp.broadcast_to(share[None], (groups, 8, col_count)), "grp", 0, 0)
    return full.reshape(groups * 8, col_count)


def solution(mesh):
    return jax.shard_map(
        body,
        mesh=mesh,
        in_specs=(P(AXES, None), P(AXES), P(AXES), P(AXES)),
        out_specs=P("row", None),
        check_vma=False,
    )
```

```python
import functools
import itertools
import math

import jax
import jax.numpy as jnp
from jax import lax
from jax.experimental import pallas as pl
from jax.experimental.pallas import tpu as pltpu
from jax.sharding import PartitionSpec as P

SKETCH = 2048
MIB = 1 << 20
LANES = 128
AXES = ("grp", "row")


def parity(bits):
    for shift in (8, 4, 2, 1):
        bits = bits ^ bits >> shift
    return bits & 1


def hadamard_sign(rows, cols):
    return (1 - 2 * parity(rows & cols)).astype(jnp.float32)


def two_parts(value):
    high = value.astype(jnp.bfloat16)
    low = (value - high.astype(jnp.float32)).astype(jnp.bfloat16)
    return high, low


def transform_kernel(cuts, place_ref, matrix_hbm, signs_hbm, own_ref, send_ref, matrix_ref, signs_ref, sems, signs_sem):
    block = matrix_ref.shape[1]
    half = block // 2
    signs_copy = pltpu.make_async_copy(signs_hbm, signs_ref, signs_sem)
    signs_copy.start()
    copies = []
    for part, (first, last) in enumerate(itertools.pairwise(cuts)):
        span = pl.ds(first, last - first)
        copies.append(pltpu.make_async_copy(matrix_hbm.at[span], matrix_ref.at[span], sems.at[part]))
        copies[-1].start()
    core = place_ref[0] & 1
    out_row = lax.broadcasted_iota(jnp.int32, (block, block), 0)
    in_row = lax.broadcasted_iota(jnp.int32, (block, block), 1)
    hadamard = hadamard_sign(out_row ^ core * half, in_row).astype(jnp.bfloat16)
    signs_copy.wait()
    for copy, (first, last) in zip(copies, itertools.pairwise(cuts)):
        copy.wait()
        for unit in range(first, last):
            high, low = two_parts(matrix_ref[unit])
            signed = hadamard * signs_ref[pl.ds(unit, 1), :].astype(jnp.float32).astype(jnp.bfloat16)
            result = jnp.dot(
                jnp.concatenate([signed, signed], axis=1),
                jnp.concatenate([high, low], axis=0),
                preferred_element_type=jnp.float32,
            )
            own_ref[unit] = result[:half]
            send_ref[unit] = result[half:]


def transform(place, matrix, row_signs):
    count, block, cols = matrix.shape
    cuts = (0, count // 4, count * 5 // 8, count)
    half = jax.ShapeDtypeStruct((count, block // 2, cols), jnp.float32)
    hbm = pl.BlockSpec(memory_space=pltpu.HBM)
    vmem = pl.BlockSpec(memory_space=pltpu.VMEM)
    return pl.pallas_call(
        functools.partial(transform_kernel, cuts),
        in_specs=[pl.BlockSpec(memory_space=pltpu.SMEM), hbm, hbm],
        out_specs=[vmem, vmem],
        out_shape=[half, half],
        scratch_shapes=[
            pltpu.VMEM(matrix.shape, jnp.float32),
            pltpu.VMEM((count, block), jnp.int32),
            pltpu.SemaphoreType.DMA((len(cuts) - 1,)),
            pltpu.SemaphoreType.DMA,
        ],
        compiler_params=pltpu.CompilerParams(vmem_limit_bytes=16 * MIB),
        cost_estimate=pl.CostEstimate(flops=2 * 2 * 128 * 128 * 256 * 32, bytes_accessed=8 * MIB, transcendentals=0),
        name="transform",
    )(
        place,
        pltpu.with_memory_space_constraint(matrix, pltpu.HBM),
        pltpu.with_memory_space_constraint(row_signs, pltpu.HBM),
    )


def mix_kernel(scale, place_ref, meta_ref, own_ref, other_ref, out_ref):
    near, _, low_count, far, rows, cols = out_ref.shape
    chips = meta_ref.shape[0]
    units = own_ref.shape[0]
    sources = 2 * chips
    targets = near * far
    me = place_ref[0] % sources
    core = me & 1
    first_x = jnp.where(core == 0, me >> 1, 0)
    first_y = jnp.where(core == 0, 0, place_ref[0] // sources // low_count)
    index = lax.broadcasted_iota(jnp.int32, (targets, units), 0)
    target = index % far * near + (index // far + first_x) % near
    same, different = (jnp.zeros((targets, units), jnp.float32) for _ in range(2))
    for source in range(chips):
        flip = 1 - 2 * parity((me >> 1) & source)
        dests, signs, other_dests, other_signs = (meta_ref[source, row : row + 1, :units] for row in range(4))
        same = same + jnp.where(dests == target, (signs * flip).astype(jnp.float32), 0.0)
        different = different + jnp.where(other_dests == target, (other_signs * flip).astype(jnp.float32), 0.0)
    side = (1 - 2 * core).astype(jnp.float32)
    tall, wide = targets * rows, units * rows
    unit_row = lax.broadcasted_iota(jnp.int32, (units, wide), 0)
    unit_col = lax.broadcasted_iota(jnp.int32, (units, wide), 1)
    spread = (hadamard_sign(unit_row, unit_col // rows) * scale).astype(jnp.bfloat16)
    keep = lax.broadcasted_iota(jnp.int32, (tall, wide), 0) % rows == lax.broadcasted_iota(jnp.int32, (tall, wide), 1) % rows
    highs, lows = [], []
    for total in (side * same + different, same - side * different):
        total = jnp.broadcast_to(total[:, None, :], (targets, rows, units)).reshape(tall, units)
        weights = jnp.dot(total.astype(jnp.bfloat16), spread, preferred_element_type=jnp.float32)
        high, low = two_parts(jnp.where(keep, weights, 0.0))
        highs.append(high)
        lows.append(low)
    left = jnp.concatenate(highs, axis=1)
    stacked = jnp.concatenate([left, jnp.concatenate(lows, axis=1)], axis=0)
    for step, low_z in itertools.product(range(near), range(low_count)):
        piece = (first_y + step) % near * low_count + low_z
        span = pl.ds(pl.multiple_of(piece * rows, rows), rows)
        parts = [two_parts(ref[:, span, :].reshape(wide, cols)) for ref in (own_ref, other_ref)]
        high, low = (jnp.concatenate(each, axis=0) for each in zip(*parts))
        both = jnp.dot(stacked, high, preferred_element_type=jnp.float32)
        result = jnp.dot(left, low, preferred_element_type=jnp.float32) + (both[:tall] + both[tall:])
        result = result.reshape(near, far, rows, cols)
        for turn in range(near):
            out_ref[jnp.where(core == 0, turn, step), jnp.where(core == 0, step, turn), low_z] = result[turn]


def mix(scale, place, meta, own, other, near, low_count, far):
    units, half, cols = own.shape
    rows = half // (near * low_count)
    vmem = pl.BlockSpec(memory_space=pltpu.VMEM)
    return pl.pallas_call(
        functools.partial(mix_kernel, scale),
        in_specs=[pl.BlockSpec(memory_space=pltpu.SMEM), vmem, vmem, vmem],
        out_specs=vmem,
        out_shape=jax.ShapeDtypeStruct((near, near, low_count, far, rows, cols), jnp.float32),
        compiler_params=pltpu.CompilerParams(vmem_limit_bytes=24 * MIB),
        cost_estimate=pl.CostEstimate(flops=2 * 3 * 128 * 512 * 256 * 8, bytes_accessed=5 * MIB, transcendentals=0),
        name="mix",
    )(place, meta, own, other)


Y, Z_LOW, Z_HIGH, X, CORE = 4, 2, 4, 4, 2


def flat_index(y, z_low, z_high, x, core):
    return (((y % Y * Z_LOW + z_low) * Z_HIGH + z_high) * X + x % X) * CORE + core


def places():
    return itertools.product(range(Y), range(Z_LOW), range(Z_HIGH), range(X), range(CORE))


def first_shift(value, step):
    pairs = []
    for y, z_low, z_high, x, core in places():
        to = (y, z_low, z_high, x + step, core) if core == 0 else (y + step, z_low, z_high, x, core)
        pairs.append((flat_index(y, z_low, z_high, x, core), flat_index(*to)))
    return lax.ppermute(value, AXES, pairs)


def second_groups():
    groups = []
    for core, fixed in itertools.product(range(CORE), range(X)):
        members = itertools.product(range(Y), range(Z_LOW), range(Z_HIGH))
        groups.append(
            [
                flat_index(free, z_low, z_high, fixed, core) if core == 0 else flat_index(fixed, z_low, z_high, free, core)
                for free, z_low, z_high in members
            ]
        )
    return groups


def body(matrix, row_signs, block_dest, block_signs):
    row_count, col_count = matrix.shape
    units = block_dest.shape[0]
    block = row_count // units
    groups = lax.axis_size("grp")
    devs = lax.axis_size("row")
    total_rows = row_count * devs * groups
    scale = math.sqrt(SKETCH / total_rows) / math.sqrt(row_count * devs)
    place = lax.axis_index(AXES).astype(jnp.int32).reshape(1)

    cores = [(i, i ^ 1) for i in range(devs)]
    swapped = [lax.ppermute(value, "row", cores) for value in (block_dest, block_signs)]
    mine = jnp.pad(jnp.stack([block_dest, block_signs, *swapped]), ((0, 0), (0, LANES - units)))
    same_core = [list(range(core, devs, CORE)) for core in range(CORE)]
    matrix = matrix.reshape(units, block, col_count)
    own, send = transform(place, matrix, row_signs.reshape(units, block))
    send, mine = lax.optimization_barrier((send, mine))
    other = lax.ppermute(send, "row", cores)
    meta = jnp.broadcast_to(mine[None], (devs // CORE, *mine.shape))
    meta = lax.all_to_all(meta, "row", 0, 0, axis_index_groups=same_core)
    parts = mix(scale, place, meta, own, other, X, Z_LOW, Z_HIGH)

    got = {step: first_shift(parts[step], step) for step in (2, 1, 3)}
    part = (parts[0] + got[2]) + (got[1] + got[3])
    pieces = part.reshape(-1, 8, col_count)
    pieces = lax.all_to_all(pieces, AXES, 0, 0, axis_index_groups=second_groups())
    share = jnp.sum(pieces, axis=0)
    full = lax.all_to_all(jnp.broadcast_to(share[None], (groups, 8, col_count)), "grp", 0, 0)
    return full.reshape(groups * 8, col_count)


def solution(mesh):
    return jax.shard_map(
        body,
        mesh=mesh,
        in_specs=(P(AXES, None), P(AXES), P(AXES), P(AXES)),
        out_specs=P("row", None),
        check_vma=False,
    )
```

```python
import functools
import itertools
import math

import jax
import jax.numpy as jnp
from jax import lax
from jax.experimental import pallas as pl
from jax.experimental.pallas import tpu as pltpu
from jax.sharding import PartitionSpec as P

SKETCH = 2048
MIB = 1 << 20
LANES = 128
AXES = ("grp", "row")


def parity(bits):
    for shift in (8, 4, 2, 1):
        bits = bits ^ bits >> shift
    return bits & 1


def hadamard_sign(rows, cols):
    return (1 - 2 * parity(rows & cols)).astype(jnp.float32)


def two_parts(value):
    high = value.astype(jnp.bfloat16)
    low = (value - high.astype(jnp.float32)).astype(jnp.bfloat16)
    return high, low


def transform_kernel(cuts, place_ref, matrix_hbm, signs_hbm, own_ref, send_ref, matrix_ref, signs_ref, sems, signs_sem):
    block = matrix_ref.shape[1]
    half = block // 2
    signs_copy = pltpu.make_async_copy(signs_hbm, signs_ref, signs_sem)
    signs_copy.start()
    copies = []
    for part, (first, last) in enumerate(itertools.pairwise(cuts)):
        span = pl.ds(first, last - first)
        copies.append(pltpu.make_async_copy(matrix_hbm.at[span], matrix_ref.at[span], sems.at[part]))
        copies[-1].start()
    core = place_ref[0] & 1
    out_row = lax.broadcasted_iota(jnp.int32, (block, block), 0)
    in_row = lax.broadcasted_iota(jnp.int32, (block, block), 1)
    hadamard = hadamard_sign(out_row ^ core * half, in_row).astype(jnp.bfloat16)
    signs_copy.wait()
    for copy, (first, last) in zip(copies, itertools.pairwise(cuts)):
        copy.wait()
        for unit in range(first, last):
            high, low = two_parts(matrix_ref[unit])
            signed = hadamard * signs_ref[pl.ds(unit, 1), :].astype(jnp.float32).astype(jnp.bfloat16)
            result = jnp.dot(
                jnp.concatenate([signed, signed], axis=1),
                jnp.concatenate([high, low], axis=0),
                preferred_element_type=jnp.float32,
            )
            own_ref[unit] = result[:half]
            send_ref[unit] = result[half:]


def transform(place, matrix, row_signs):
    count, block, cols = matrix.shape
    cuts = (0, count // 4, count * 5 // 8, count)
    half = jax.ShapeDtypeStruct((count, block // 2, cols), jnp.float32)
    hbm = pl.BlockSpec(memory_space=pltpu.HBM)
    vmem = pl.BlockSpec(memory_space=pltpu.VMEM)
    return pl.pallas_call(
        functools.partial(transform_kernel, cuts),
        in_specs=[pl.BlockSpec(memory_space=pltpu.SMEM), hbm, hbm],
        out_specs=[vmem, vmem],
        out_shape=[half, half],
        scratch_shapes=[
            pltpu.VMEM(matrix.shape, jnp.float32),
            pltpu.VMEM((count, block), jnp.int32),
            pltpu.SemaphoreType.DMA((len(cuts) - 1,)),
            pltpu.SemaphoreType.DMA,
        ],
        compiler_params=pltpu.CompilerParams(vmem_limit_bytes=16 * MIB),
        cost_estimate=pl.CostEstimate(flops=2 * 2 * 128 * 128 * 256 * 32, bytes_accessed=8 * MIB, transcendentals=0),
        name="transform",
    )(
        place,
        pltpu.with_memory_space_constraint(matrix, pltpu.HBM),
        pltpu.with_memory_space_constraint(row_signs, pltpu.HBM),
    )


def mix_kernel(scale, place_ref, meta_ref, own_ref, other_ref, out_ref):
    near, _, low_count, far, rows, cols = out_ref.shape
    chips = meta_ref.shape[0]
    units = own_ref.shape[0]
    sources = 2 * chips
    targets = near * far
    me = place_ref[0] % sources
    core = me & 1
    first_x = jnp.where(core == 0, me >> 1, 0)
    first_y = jnp.where(core == 0, 0, place_ref[0] // sources // low_count)
    index = lax.broadcasted_iota(jnp.int32, (targets, units), 0)
    target = index % far * near + (index // far + first_x) % near
    same, different = (jnp.zeros((targets, units), jnp.float32) for _ in range(2))
    for source in range(chips):
        flip = 1 - 2 * parity((me >> 1) & source)
        dests, signs, other_dests, other_signs = (meta_ref[source, row : row + 1, :units] for row in range(4))
        same = same + jnp.where(dests == target, (signs * flip).astype(jnp.float32), 0.0)
        different = different + jnp.where(other_dests == target, (other_signs * flip).astype(jnp.float32), 0.0)
    side = (1 - 2 * core).astype(jnp.float32)
    tall, wide = targets * rows, units * rows
    unit_row = lax.broadcasted_iota(jnp.int32, (units, wide), 0)
    unit_col = lax.broadcasted_iota(jnp.int32, (units, wide), 1)
    spread = (hadamard_sign(unit_row, unit_col // rows) * scale).astype(jnp.bfloat16)
    keep = lax.broadcasted_iota(jnp.int32, (tall, wide), 0) % rows == lax.broadcasted_iota(jnp.int32, (tall, wide), 1) % rows
    totals = jnp.concatenate([side * same + different, same - side * different], axis=0)
    totals = jnp.broadcast_to(totals[:, None, :], (2 * targets, rows, units)).reshape(2 * tall, units)
    weights = jnp.dot(totals.astype(jnp.bfloat16), spread, preferred_element_type=jnp.float32)
    weights = jnp.concatenate([jnp.where(keep, weights[:tall], 0.0), jnp.where(keep, weights[tall:], 0.0)], axis=1)
    left, low_left = two_parts(weights)
    stacked = jnp.concatenate([left, low_left], axis=0)
    for step, low_z in itertools.product(range(near), range(low_count)):
        piece = (first_y + step) % near * low_count + low_z
        span = pl.ds(pl.multiple_of(piece * rows, rows), rows)
        parts = [two_parts(ref[:, span, :].reshape(wide, cols)) for ref in (own_ref, other_ref)]
        high, low = (jnp.concatenate(each, axis=0) for each in zip(*parts))
        both = jnp.dot(stacked, high, preferred_element_type=jnp.float32)
        result = jnp.dot(left, low, preferred_element_type=jnp.float32) + (both[:tall] + both[tall:])
        result = result.reshape(near, far, rows, cols)
        for turn in range(near):
            out_ref[jnp.where(core == 0, turn, step), jnp.where(core == 0, step, turn), low_z] = result[turn]


def mix(scale, place, meta, own, other, near, low_count, far):
    units, half, cols = own.shape
    rows = half // (near * low_count)
    vmem = pl.BlockSpec(memory_space=pltpu.VMEM)
    return pl.pallas_call(
        functools.partial(mix_kernel, scale),
        in_specs=[pl.BlockSpec(memory_space=pltpu.SMEM), vmem, vmem, vmem],
        out_specs=vmem,
        out_shape=jax.ShapeDtypeStruct((near, near, low_count, far, rows, cols), jnp.float32),
        compiler_params=pltpu.CompilerParams(vmem_limit_bytes=24 * MIB),
        cost_estimate=pl.CostEstimate(flops=2 * 3 * 128 * 512 * 256 * 8, bytes_accessed=5 * MIB, transcendentals=0),
        name="mix",
    )(place, meta, own, other)


Y, Z_LOW, Z_HIGH, X, CORE = 4, 2, 4, 4, 2


def flat_index(y, z_low, z_high, x, core):
    return (((y % Y * Z_LOW + z_low) * Z_HIGH + z_high) * X + x % X) * CORE + core


def places():
    return itertools.product(range(Y), range(Z_LOW), range(Z_HIGH), range(X), range(CORE))


def first_shift(value, step):
    pairs = []
    for y, z_low, z_high, x, core in places():
        to = (y, z_low, z_high, x + step, core) if core == 0 else (y + step, z_low, z_high, x, core)
        pairs.append((flat_index(y, z_low, z_high, x, core), flat_index(*to)))
    return lax.ppermute(value, AXES, pairs)


def second_groups():
    groups = []
    for core, fixed in itertools.product(range(CORE), range(X)):
        members = itertools.product(range(Y), range(Z_LOW), range(Z_HIGH))
        groups.append(
            [
                flat_index(free, z_low, z_high, fixed, core) if core == 0 else flat_index(fixed, z_low, z_high, free, core)
                for free, z_low, z_high in members
            ]
        )
    return groups


def body(matrix, row_signs, block_dest, block_signs):
    row_count, col_count = matrix.shape
    units = block_dest.shape[0]
    block = row_count // units
    groups = lax.axis_size("grp")
    devs = lax.axis_size("row")
    total_rows = row_count * devs * groups
    scale = math.sqrt(SKETCH / total_rows) / math.sqrt(row_count * devs)
    place = lax.axis_index(AXES).astype(jnp.int32).reshape(1)

    cores = [(i, i ^ 1) for i in range(devs)]
    swapped = [lax.ppermute(value, "row", cores) for value in (block_dest, block_signs)]
    mine = jnp.pad(jnp.stack([block_dest, block_signs, *swapped]), ((0, 0), (0, LANES - units)))
    same_core = [list(range(core, devs, CORE)) for core in range(CORE)]
    matrix = matrix.reshape(units, block, col_count)
    own, send = transform(place, matrix, row_signs.reshape(units, block))
    send, mine = lax.optimization_barrier((send, mine))
    other = lax.ppermute(send, "row", cores)
    meta = jnp.broadcast_to(mine[None], (devs // CORE, *mine.shape))
    meta = lax.all_to_all(meta, "row", 0, 0, axis_index_groups=same_core)
    parts = mix(scale, place, meta, own, other, X, Z_LOW, Z_HIGH)

    got = {step: first_shift(parts[step], step) for step in (2, 1, 3)}
    part = (parts[0] + got[2]) + (got[1] + got[3])
    pieces = part.reshape(-1, 8, col_count)
    pieces = lax.all_to_all(pieces, AXES, 0, 0, axis_index_groups=second_groups())
    share = jnp.sum(pieces, axis=0)
    full = lax.all_to_all(jnp.broadcast_to(share[None], (groups, 8, col_count)), "grp", 0, 0)
    return full.reshape(groups * 8, col_count)


def solution(mesh):
    return jax.shard_map(
        body,
        mesh=mesh,
        in_specs=(P(AXES, None), P(AXES), P(AXES), P(AXES)),
        out_specs=P("row", None),
        check_vma=False,
    )
```

```python
import functools
import itertools
import math

import jax
import jax.numpy as jnp
from jax import lax
from jax.experimental import pallas as pl
from jax.experimental.pallas import tpu as pltpu
from jax.sharding import PartitionSpec as P

SKETCH = 2048
MIB = 1 << 20
AXES = ("grp", "row")


def parity(bits):
    for shift in (8, 4, 2, 1):
        bits = bits ^ bits >> shift
    return bits & 1


def hadamard_sign(rows, cols):
    return (1 - 2 * parity(rows & cols)).astype(jnp.float32)


def two_parts(value):
    high = value.astype(jnp.bfloat16)
    low = (value - high.astype(jnp.float32)).astype(jnp.bfloat16)
    return high, low


def transform_kernel(cuts, place_ref, matrix_hbm, signs_hbm, own_ref, send_ref, matrix_ref, signs_ref, sems, signs_sem):
    block = matrix_ref.shape[1]
    half = block // 2
    signs_copy = pltpu.make_async_copy(signs_hbm, signs_ref, signs_sem)
    signs_copy.start()
    copies = []
    for part, (first, last) in enumerate(itertools.pairwise(cuts)):
        span = pl.ds(first, last - first)
        copies.append(pltpu.make_async_copy(matrix_hbm.at[span], matrix_ref.at[span], sems.at[part]))
        copies[-1].start()
    core = place_ref[0] & 1
    out_row = lax.broadcasted_iota(jnp.int32, (block, block), 0)
    in_row = lax.broadcasted_iota(jnp.int32, (block, block), 1)
    hadamard = hadamard_sign(out_row ^ core * half, in_row).astype(jnp.bfloat16)
    signs_copy.wait()
    for copy, (first, last) in zip(copies, itertools.pairwise(cuts)):
        copy.wait()
        for unit in range(first, last):
            high, low = two_parts(matrix_ref[unit])
            signed = hadamard * signs_ref[pl.ds(unit, 1), :].astype(jnp.float32).astype(jnp.bfloat16)
            result = jnp.dot(
                jnp.concatenate([signed, signed], axis=1),
                jnp.concatenate([high, low], axis=0),
                preferred_element_type=jnp.float32,
            )
            own_ref[unit] = result[:half]
            send_ref[unit] = result[half:]


def transform(place, matrix, row_signs):
    count, block, cols = matrix.shape
    cuts = (0, count // 4, count * 5 // 8, count)
    half = jax.ShapeDtypeStruct((count, block // 2, cols), jnp.float32)
    hbm = pl.BlockSpec(memory_space=pltpu.HBM)
    vmem = pl.BlockSpec(memory_space=pltpu.VMEM)
    return pl.pallas_call(
        functools.partial(transform_kernel, cuts),
        in_specs=[pl.BlockSpec(memory_space=pltpu.SMEM), hbm, hbm],
        out_specs=[vmem, vmem],
        out_shape=[half, half],
        scratch_shapes=[
            pltpu.VMEM(matrix.shape, jnp.float32),
            pltpu.VMEM((count, block), jnp.int32),
            pltpu.SemaphoreType.DMA((len(cuts) - 1,)),
            pltpu.SemaphoreType.DMA,
        ],
        compiler_params=pltpu.CompilerParams(vmem_limit_bytes=16 * MIB),
        cost_estimate=pl.CostEstimate(flops=2 * 2 * 128 * 128 * 256 * 32, bytes_accessed=8 * MIB, transcendentals=0),
        name="transform",
    )(
        place,
        pltpu.with_memory_space_constraint(matrix, pltpu.HBM),
        pltpu.with_memory_space_constraint(row_signs, pltpu.HBM),
    )


def mix_kernel(scale, place_ref, meta_ref, own_ref, other_ref, out_ref):
    near, _, low_count, far, rows, cols = out_ref.shape
    sources, _, units = meta_ref.shape
    targets = near * far
    me = place_ref[0] % sources
    core = me & 1
    first_x = jnp.where(core == 1, me >> 1, 0)
    first_y = jnp.where(core == 1, 0, place_ref[0] // sources // low_count)
    index = lax.broadcasted_iota(jnp.int32, (targets, units), 0)
    target = index % far * near + (index // far + first_x) % near
    sums = [jnp.zeros((targets, units), jnp.float32) for _ in range(2)]
    for source in range(sources):
        flip = 1 - 2 * parity((me >> 1) & (source >> 1))
        dests = meta_ref[source, 0:1, :]
        signs = meta_ref[source, 1:2, :] * flip
        routed = jnp.where(dests == target, signs.astype(jnp.float32), 0.0)
        sums[source & 1] = sums[source & 1] + routed
    side = (1 - 2 * core).astype(jnp.float32)
    tall, wide = targets * rows, units * rows
    unit_row = lax.broadcasted_iota(jnp.int32, (units, wide), 0)
    unit_col = lax.broadcasted_iota(jnp.int32, (units, wide), 1)
    spread = (hadamard_sign(unit_row, unit_col // rows) * scale).astype(jnp.bfloat16)
    keep = lax.broadcasted_iota(jnp.int32, (tall, wide), 0) % rows == lax.broadcasted_iota(jnp.int32, (tall, wide), 1) % rows
    highs, lows = [], []
    for total in (sums[0] + side * sums[1], sums[0] - side * sums[1]):
        total = jnp.broadcast_to(total[:, None, :], (targets, rows, units)).reshape(tall, units)
        weights = jnp.dot(total.astype(jnp.bfloat16), spread, preferred_element_type=jnp.float32)
        high, low = two_parts(jnp.where(keep, weights, 0.0))
        highs.append(high)
        lows.append(low)
    left = jnp.concatenate(highs, axis=1)
    stacked = jnp.concatenate([left, jnp.concatenate(lows, axis=1)], axis=0)
    for step, low_z in itertools.product(range(near), range(low_count)):
        piece = (first_y + step) % near * low_count + low_z
        span = pl.ds(pl.multiple_of(piece * rows, rows), rows)
        parts = [two_parts(ref[:, span, :].reshape(wide, cols)) for ref in (own_ref, other_ref)]
        high, low = (jnp.concatenate(each, axis=0) for each in zip(*parts))
        both = jnp.dot(stacked, high, preferred_element_type=jnp.float32)
        result = jnp.dot(left, low, preferred_element_type=jnp.float32) + (both[:tall] + both[tall:])
        result = result.reshape(near, far, rows, cols)
        for turn in range(near):
            out_ref[jnp.where(core == 1, turn, step), jnp.where(core == 1, step, turn), low_z] = result[turn]


def mix(scale, place, meta, own, other, near, low_count, far):
    units, half, cols = own.shape
    rows = half // (near * low_count)
    vmem = pl.BlockSpec(memory_space=pltpu.VMEM)
    return pl.pallas_call(
        functools.partial(mix_kernel, scale),
        in_specs=[pl.BlockSpec(memory_space=pltpu.SMEM), vmem, vmem, vmem],
        out_specs=vmem,
        out_shape=jax.ShapeDtypeStruct((near, near, low_count, far, rows, cols), jnp.float32),
        compiler_params=pltpu.CompilerParams(vmem_limit_bytes=24 * MIB),
        cost_estimate=pl.CostEstimate(flops=2 * 3 * 128 * 512 * 256 * 8, bytes_accessed=5 * MIB, transcendentals=0),
        name="mix",
    )(place, meta, own, other)


Y, Z_LOW, Z_HIGH, X, CORE = 4, 2, 4, 4, 2


def flat_index(y, z_low, z_high, x, core):
    return (((y % Y * Z_LOW + z_low) * Z_HIGH + z_high) * X + x % X) * CORE + core


def places():
    return itertools.product(range(Y), range(Z_LOW), range(Z_HIGH), range(X), range(CORE))


def first_shift(value, step):
    pairs = []
    for y, z_low, z_high, x, core in places():
        to = (y, z_low, z_high, x + step, core) if core == 1 else (y + step, z_low, z_high, x, core)
        pairs.append((flat_index(y, z_low, z_high, x, core), flat_index(*to)))
    return lax.ppermute(value, AXES, pairs)


def second_groups():
    groups = []
    for core, fixed in itertools.product(range(CORE), range(X)):
        members = itertools.product(range(Y), range(Z_LOW), range(Z_HIGH))
        groups.append(
            [
                flat_index(free, z_low, z_high, fixed, core) if core == 1 else flat_index(fixed, z_low, z_high, free, core)
                for free, z_low, z_high in members
            ]
        )
    return groups


def body(matrix, row_signs, block_dest, block_signs):
    row_count, col_count = matrix.shape
    units = block_dest.shape[0]
    block = row_count // units
    groups = lax.axis_size("grp")
    devs = lax.axis_size("row")
    total_rows = row_count * devs * groups
    scale = math.sqrt(SKETCH / total_rows) / math.sqrt(row_count * devs)
    place = lax.axis_index(AXES).astype(jnp.int32).reshape(1)

    mine = jnp.stack([block_dest, block_signs])
    meta = lax.all_to_all(jnp.broadcast_to(mine[None], (devs, 2, units)), "row", 0, 0)
    matrix = matrix.reshape(units, block, col_count)
    row_signs = row_signs.reshape(units, block)
    own, send = transform(place, matrix, row_signs)
    other = lax.ppermute(send, "row", [(i, i ^ 1) for i in range(devs)])
    parts = mix(scale, place, meta, own, other, X, Z_LOW, Z_HIGH)

    got = {step: first_shift(parts[step], step) for step in (2, 1, 3)}
    part = (parts[0] + got[2]) + (got[1] + got[3])
    pieces = part.reshape(-1, 8, col_count)
    pieces = lax.all_to_all(pieces, AXES, 0, 0, axis_index_groups=second_groups())
    share = jnp.sum(pieces, axis=0)
    full = lax.all_to_all(jnp.broadcast_to(share[None], (groups, 8, col_count)), "grp", 0, 0)
    return full.reshape(groups * 8, col_count)


def solution(mesh):
    return jax.shard_map(
        body,
        mesh=mesh,
        in_specs=(P(AXES, None), P(AXES), P(AXES), P(AXES)),
        out_specs=P("row", None),
        check_vma=False,
    )
```

```python
import functools
import itertools
import math

import jax
import jax.numpy as jnp
from jax import lax
from jax.experimental import pallas as pl
from jax.experimental.pallas import tpu as pltpu
from jax.sharding import PartitionSpec as P

SKETCH = 2048
MIB = 1 << 20
AXES = ("grp", "row")


def parity(bits):
    for shift in (8, 4, 2, 1):
        bits = bits ^ bits >> shift
    return bits & 1


def hadamard_sign(rows, cols):
    return (1 - 2 * parity(rows & cols)).astype(jnp.float32)


def two_parts(value):
    high = value.astype(jnp.bfloat16)
    low = (value - high.astype(jnp.float32)).astype(jnp.bfloat16)
    return high, low


def transform_kernel(cuts, place_ref, matrix_hbm, signs_hbm, own_ref, send_ref, matrix_ref, signs_ref, sems, signs_sem):
    block = matrix_ref.shape[1]
    half = block // 2
    signs_copy = pltpu.make_async_copy(signs_hbm, signs_ref, signs_sem)
    signs_copy.start()
    copies = []
    for part, (first, last) in enumerate(itertools.pairwise(cuts)):
        span = pl.ds(first, last - first)
        copies.append(pltpu.make_async_copy(matrix_hbm.at[span], matrix_ref.at[span], sems.at[part]))
        copies[-1].start()
    core = place_ref[0] & 1
    out_row = lax.broadcasted_iota(jnp.int32, (block, block), 0)
    in_row = lax.broadcasted_iota(jnp.int32, (block, block), 1)
    hadamard = hadamard_sign(out_row ^ core * half, in_row).astype(jnp.bfloat16)
    signs_copy.wait()
    for copy, (first, last) in zip(copies, itertools.pairwise(cuts)):
        copy.wait()
        for unit in range(first, last):
            high, low = two_parts(matrix_ref[unit])
            signed = hadamard * signs_ref[pl.ds(unit, 1), :].astype(jnp.float32).astype(jnp.bfloat16)
            result = jnp.dot(
                jnp.concatenate([signed, signed], axis=1),
                jnp.concatenate([high, low], axis=0),
                preferred_element_type=jnp.float32,
            )
            own_ref[unit] = result[:half]
            send_ref[unit] = result[half:]


def transform(place, matrix, row_signs):
    count, block, cols = matrix.shape
    cuts = (0, count // 4, count * 11 // 16, count)
    half = jax.ShapeDtypeStruct((count, block // 2, cols), jnp.float32)
    hbm = pl.BlockSpec(memory_space=pltpu.HBM)
    vmem = pl.BlockSpec(memory_space=pltpu.VMEM)
    return pl.pallas_call(
        functools.partial(transform_kernel, cuts),
        in_specs=[pl.BlockSpec(memory_space=pltpu.SMEM), hbm, hbm],
        out_specs=[vmem, vmem],
        out_shape=[half, half],
        scratch_shapes=[
            pltpu.VMEM(matrix.shape, jnp.float32),
            pltpu.VMEM((count, block), jnp.int32),
            pltpu.SemaphoreType.DMA((len(cuts) - 1,)),
            pltpu.SemaphoreType.DMA,
        ],
        compiler_params=pltpu.CompilerParams(vmem_limit_bytes=16 * MIB),
        cost_estimate=pl.CostEstimate(flops=2 * 2 * 128 * 128 * 256 * 32, bytes_accessed=8 * MIB, transcendentals=0),
        name="transform",
    )(
        place,
        pltpu.with_memory_space_constraint(matrix, pltpu.HBM),
        pltpu.with_memory_space_constraint(row_signs, pltpu.HBM),
    )


def mix_kernel(scale, place_ref, meta_ref, own_ref, other_ref, out_ref):
    near, _, low_count, far, rows, cols = out_ref.shape
    sources, _, units = meta_ref.shape
    targets = near * far
    me = place_ref[0] % sources
    core = me & 1
    first_x = jnp.where(core == 0, me >> 1, 0)
    first_y = jnp.where(core == 0, 0, place_ref[0] // sources // low_count)
    index = lax.broadcasted_iota(jnp.int32, (targets, units), 0)
    target = index % far * near + (index // far + first_x) % near
    sums = [jnp.zeros((targets, units), jnp.float32) for _ in range(2)]
    for source in range(sources):
        flip = 1 - 2 * parity((me >> 1) & (source >> 1))
        dests = meta_ref[source, 0:1, :]
        signs = meta_ref[source, 1:2, :] * flip
        routed = jnp.where(dests == target, signs.astype(jnp.float32), 0.0)
        sums[source & 1] = sums[source & 1] + routed
    side = (1 - 2 * core).astype(jnp.float32)
    tall, wide = targets * rows, units * rows
    unit_row = lax.broadcasted_iota(jnp.int32, (units, wide), 0)
    unit_col = lax.broadcasted_iota(jnp.int32, (units, wide), 1)
    spread = (hadamard_sign(unit_row, unit_col // rows) * scale).astype(jnp.bfloat16)
    keep = lax.broadcasted_iota(jnp.int32, (tall, wide), 0) % rows == lax.broadcasted_iota(jnp.int32, (tall, wide), 1) % rows
    highs, lows = [], []
    for total in (sums[0] + side * sums[1], sums[0] - side * sums[1]):
        total = jnp.broadcast_to(total[:, None, :], (targets, rows, units)).reshape(tall, units)
        weights = jnp.dot(total.astype(jnp.bfloat16), spread, preferred_element_type=jnp.float32)
        high, low = two_parts(jnp.where(keep, weights, 0.0))
        highs.append(high)
        lows.append(low)
    left = jnp.concatenate(highs, axis=1)
    stacked = jnp.concatenate([left, jnp.concatenate(lows, axis=1)], axis=0)
    for step, low_z in itertools.product(range(near), range(low_count)):
        piece = (first_y + step) % near * low_count + low_z
        span = pl.ds(pl.multiple_of(piece * rows, rows), rows)
        parts = [two_parts(ref[:, span, :].reshape(wide, cols)) for ref in (own_ref, other_ref)]
        high, low = (jnp.concatenate(each, axis=0) for each in zip(*parts))
        both = jnp.dot(stacked, high, preferred_element_type=jnp.float32)
        result = jnp.dot(left, low, preferred_element_type=jnp.float32) + (both[:tall] + both[tall:])
        result = result.reshape(near, far, rows, cols)
        for turn in range(near):
            out_ref[jnp.where(core == 0, turn, step), jnp.where(core == 0, step, turn), low_z] = result[turn]


def mix(scale, place, meta, own, other, near, low_count, far):
    units, half, cols = own.shape
    rows = half // (near * low_count)
    vmem = pl.BlockSpec(memory_space=pltpu.VMEM)
    return pl.pallas_call(
        functools.partial(mix_kernel, scale),
        in_specs=[pl.BlockSpec(memory_space=pltpu.SMEM), vmem, vmem, vmem],
        out_specs=vmem,
        out_shape=jax.ShapeDtypeStruct((near, near, low_count, far, rows, cols), jnp.float32),
        compiler_params=pltpu.CompilerParams(vmem_limit_bytes=24 * MIB),
        cost_estimate=pl.CostEstimate(flops=2 * 3 * 128 * 512 * 256 * 8, bytes_accessed=5 * MIB, transcendentals=0),
        name="mix",
    )(place, meta, own, other)


Y, Z_LOW, Z_HIGH, X, CORE = 4, 2, 4, 4, 2


def flat_index(y, z_low, z_high, x, core):
    return (((y % Y * Z_LOW + z_low) * Z_HIGH + z_high) * X + x % X) * CORE + core


def places():
    return itertools.product(range(Y), range(Z_LOW), range(Z_HIGH), range(X), range(CORE))


def first_shift(value, step):
    pairs = []
    for y, z_low, z_high, x, core in places():
        to = (y, z_low, z_high, x + step, core) if core == 0 else (y + step, z_low, z_high, x, core)
        pairs.append((flat_index(y, z_low, z_high, x, core), flat_index(*to)))
    return lax.ppermute(value, AXES, pairs)


def second_groups():
    groups = []
    for core, fixed in itertools.product(range(CORE), range(X)):
        members = itertools.product(range(Y), range(Z_LOW), range(Z_HIGH))
        groups.append(
            [
                flat_index(free, z_low, z_high, fixed, core) if core == 0 else flat_index(fixed, z_low, z_high, free, core)
                for free, z_low, z_high in members
            ]
        )
    return groups


def body(matrix, row_signs, block_dest, block_signs):
    row_count, col_count = matrix.shape
    units = block_dest.shape[0]
    block = row_count // units
    groups = lax.axis_size("grp")
    devs = lax.axis_size("row")
    total_rows = row_count * devs * groups
    scale = math.sqrt(SKETCH / total_rows) / math.sqrt(row_count * devs)
    place = lax.axis_index(AXES).astype(jnp.int32).reshape(1)

    mine = jnp.stack([block_dest, block_signs])
    meta = lax.all_to_all(jnp.broadcast_to(mine[None], (devs, 2, units)), "row", 0, 0)
    matrix = matrix.reshape(units, block, col_count)
    row_signs = row_signs.reshape(units, block)
    own, send = transform(place, matrix, row_signs)
    other = lax.ppermute(send, "row", [(i, i ^ 1) for i in range(devs)])
    parts = mix(scale, place, meta, own, other, X, Z_LOW, Z_HIGH)

    got = {step: first_shift(parts[step], step) for step in (2, 1, 3)}
    part = (parts[0] + got[2]) + (got[1] + got[3])
    pieces = part.reshape(-1, 8, col_count)
    pieces = lax.all_to_all(pieces, AXES, 0, 0, axis_index_groups=second_groups())
    share = jnp.sum(pieces, axis=0)
    full = lax.all_to_all(jnp.broadcast_to(share[None], (groups, 8, col_count)), "grp", 0, 0)
    return full.reshape(groups * 8, col_count)


def solution(mesh):
    return jax.shard_map(
        body,
        mesh=mesh,
        in_specs=(P(AXES, None), P(AXES), P(AXES), P(AXES)),
        out_specs=P("row", None),
        check_vma=False,
    )
```
